32 devices in a mesh: clip: 2 (over y), tile: 4 (over z), frame: 2 (over x), chan: 2 (over core).
Axes of the slice: x: 2, y: 2, z: 4, core: 2. Of those that a mesh axis runs over, the one named last changes fastest.
Arguments:
- features: bfloat16 [4, 8, 256, 256], P(('clip', 'frame'), 'tile', None, 'chan'), parts along dimension 0, may hold values from -6 to 6
- neighbours: int32 [16, 9], P(('clip', 'tile')), parts along dimension 0, may hold values from 0 to 7, as said below
- pairing: int32 [4, 2], P(('clip', 'frame')), parts along dimension 0, may hold values 0 or 1
- valid_tiles: int32 [16, 256], P(('clip', 'tile')), parts along dimension 0, may hold values 0 or 1
- cotangent: bfloat16 [4, 8, 256, 3060], P(('clip', 'frame'), 'tile', 'chan'), parts along dimension 0, may hold values from -6 to 6
Outputs:
- volume: bfloat16 [4, 8, 256, 3060], P(('clip', 'frame'), 'tile', 'chan'), parts along dimension 0
- feature_grad: float32 [4, 8, 256, 256], P(('clip', 'frame'), 'tile', None, 'chan'), parts along dimension 0
The draws below stay inside these ranges and needn't reach their ends.
There are 2 independent parts, one for each index of `clip`. The reference program is written for one: setup_inputs(seed, part) draws one part's arguments, and reference() takes and returns one part's arrays. A program takes and returns all parts, laid end to end along the dimension named above; each array names one. Nothing has to cross between parts.
Inputs may be any that keep to these rules, and one draw needn't show every extreme that they name: `neighbours`: every entry of row a lies within 2 tiles of a, and in every row one entry lies exactly 2 tiles from a.
All inputs are finite; a program needn't handle non-finite values. No bound on the sum of `pairing` or of `valid_tiles` on one device may be relied on, other than what follows from the above.
Results may differ from the reference program's by a relative error of at most 0.008.
Values may be sent and summed in bfloat16 or wider, within the bound.
No kernel may reach another device: no remote copies, remote signals or barrier semaphores. Data moves between devices by JAX's collectives and lax.ppermute only.
A program may use at most 64 MiB of HBM per device.

```python
import math
import jax
import jax.numpy as jnp
from jax import lax

CHANNELS = 256
SIDE = 16
PIXELS = 256
LEVELS = 340
NEIGHBOURS = 9
TILE_DEV = 2
TILES = 8
FRAMES = 2


def draw_neighbours(key, part):
    tile_ids = jnp.arange(TILES, dtype=jnp.int32)[:, None]
    offsets = jax.random.randint(key, (TILES, NEIGHBOURS), -TILE_DEV, TILE_DEV + 1).astype(jnp.int32)
    farthest = jnp.where(tile_ids + TILE_DEV < TILES, TILE_DEV, -TILE_DEV).astype(jnp.int32)
    offsets = offsets.at[:, 0].set(farthest[:, 0])
    return jnp.clip(tile_ids + offsets, 0, TILES - 1).astype(jnp.int32)


def with_ends(array, rng, least, high):
    longest = array.shape.index(max(array.shape))
    spots = []
    for shift in (0, 1):
        where = [jax.random.randint(jax.random.fold_in(rng, axis), (), 0, length) for axis, length in enumerate(array.shape)]
        where[longest] = (where[longest] + shift) % array.shape[longest]
        spots.append(tuple(where))
    return array.at[spots[0]].set(least).at[spots[1]].set(high)


def block_levels(own_key, dims, cuts, least, top_value):
    gain, own = 1.0, jax.random.fold_in(own_key, 6)
    for axis_at, blocks in cuts:
        heights = jnp.exp(jax.random.uniform(jax.random.fold_in(own, axis_at), (blocks,), jnp.float32, least / len(cuts), top_value / len(cuts)))
        gain = gain * jnp.repeat(heights, dims[axis_at] // blocks).reshape([-1 if axis == axis_at else 1 for axis in range(len(dims))])
    return gain


def bell_draw(own_key, shape, scale, most, split=(), kind=jnp.bfloat16):
    gain = block_levels(own_key, shape, split, -0.22, 0.18) if split else 1.0
    entries = jax.random.normal(own_key, shape, jnp.float32) * scale * gain
    return jnp.minimum(jnp.maximum(entries, -most), most).astype(kind)


def setup_inputs(seed: int = 0, part: int = 0) -> dict:
    splits = jax.random.split(jax.random.key(seed), 6)
    part_splits = jax.random.split(jax.random.fold_in(splits[5], part), 6)
    return {
        "features": bell_draw(part_splits[0], (FRAMES, TILES, PIXELS, CHANNELS), 1.0, 6.0, ((0, 2), (1, 4), (3, 2))),
        "neighbours": draw_neighbours(jax.random.fold_in(jax.random.fold_in(splits[5], part), 71), part),
        "pairing": with_ends((jax.random.randint(part_splits[2], (FRAMES, 2), 0, 4) < 3).astype(jnp.int32), jax.random.fold_in(part_splits[2], 1), 0, 1),
        "valid_tiles": with_ends((jax.random.randint(part_splits[3], (TILES, PIXELS), 0, 4) < 3).astype(jnp.int32), jax.random.fold_in(part_splits[3], 1), 0, 1),
        "cotangent": bell_draw(part_splits[4], (FRAMES, TILES, PIXELS, NEIGHBOURS * LEVELS), 1.0, 6.0, ((0, 2), (1, 4), (2, 2))),
    }


def pyramid_of(float_features):
    grid_view = float_features.reshape(FRAMES, TILES, SIDE, SIDE, CHANNELS)
    levels = []
    for extent in (1, 2, 4, 8):
        across = SIDE // extent
        pooled = grid_view.reshape(FRAMES, TILES, across, extent, across, extent, CHANNELS).mean(axis=(3, 5))
        levels.append(pooled.reshape(FRAMES, TILES, across * across, CHANNELS))
    pooled = jnp.concatenate(levels, 2)
    rounded = lax.optimization_barrier(pooled.astype(jnp.bfloat16)).astype(pooled.dtype)
    return pooled + lax.stop_gradient(rounded - pooled)

def correlate(float_features, neighbours, pairing, valid_tiles):
    pyramid = pyramid_of(float_features)
    blank_frame = jnp.zeros_like(pyramid[:1])
    before = jnp.concatenate([blank_frame, pyramid[:-1]], 0)
    following = jnp.concatenate([pyramid[1:], blank_frame], 0)
    summed = jnp.zeros((FRAMES, TILES, PIXELS, NEIGHBOURS, LEVELS), float_features.dtype)
    for partner_index, partner in enumerate((before, following)):
        chosen = partner[:, neighbours]
        scores = jnp.einsum('fapc,fakmc->fapkm', float_features, chosen, precision=lax.Precision.HIGHEST)
        gate = pairing[:, partner_index].astype(float_features.dtype)[:, None, None, None, None]
        summed = summed + gate * scores
    summed = summed * (valid_tiles.astype(float_features.dtype)[None, :, :, None, None] / math.sqrt(CHANNELS))
    return summed.reshape(FRAMES, TILES, PIXELS, NEIGHBOURS * LEVELS)

def reference(features, neighbours, pairing, valid_tiles, cotangent):
    float_features = features.astype(jnp.float32)

    def forward(values):
        return correlate(values, neighbours, pairing, valid_tiles)
    volume, pullback = jax.vjp(forward, float_features)
    feature_grad, = pullback(cotangent.astype(jnp.float32))
    return (volume.astype(jnp.bfloat16), feature_grad)
```

```python
import functools

import jax
import jax.numpy as jnp
import numpy as np
from jax import lax
from jax.experimental import pallas as pl
from jax.experimental.pallas import tpu as pltpu
from jax.sharding import PartitionSpec as P

CHANNELS = 256
SIDE = 16
PIXELS = 256
LEVELS = 340
NEIGHBOURS = 9
REACH = 2
SPAN = 2 * REACH + 1
COARSE = LEVELS - PIXELS
PAD = 128
WIDE = PIXELS + PAD

VMEM = pl.BlockSpec(memory_space=pltpu.VMEM)
SMEM = pl.BlockSpec(memory_space=pltpu.SMEM)


def coarse_weights():
    pixel = np.arange(PIXELS)
    rows, columns = pixel // SIDE, pixel % SIDE
    table = np.zeros((PAD, PIXELS), np.float32)
    base = 0
    for extent in (2, 4, 8):
        across = SIDE // extent
        cell = rows // extent * across + columns // extent
        table[base + cell, pixel] = 1.0 / (extent * extent)
        base += across * across
    return table


def even_pairs(count):
    pairs = []
    for i in range(0, count - 1, 2):
        pairs += [(i, i + 1), (i + 1, i)]
    if count % 2:
        pairs.append((count - 1, count - 1))
    return pairs


def odd_pairs(count, cores):
    pairs, paired = [], set()
    for i in range(1, count - 1, 2):
        paired |= {i, i + 1}
        for c in range(cores):
            pairs += [(i * cores + c, (i + 1) * cores + c), ((i + 1) * cores + c, i * cores + c)]
    for i in range(count):
        if i not in paired:
            pairs += [(i * cores + c, i * cores + (c + 1) % cores) for c in range(cores)]
    return pairs


def frame_links(count):
    if count == 2:
        swap = [(0, 1), (1, 0)]
        return [(swap, swap)]
    onward = [(i, i + 1) for i in range(count - 1)]
    back = [(i + 1, i) for i in range(count - 1)]
    return [(onward, back), (back, onward)]


def column_of(row):
    n = row.shape[1]
    diagonal = lax.broadcasted_iota(jnp.int32, (n, n), 0) == lax.broadcasted_iota(jnp.int32, (n, n), 1)
    return jnp.sum(jnp.where(diagonal, row, 0.0), axis=1, keepdims=True)


def valid_column(valid_ref, a, core, half):
    row = valid_ref[a : a + 1, :].astype(jnp.float32)
    return column_of(jnp.where(core == 0, row[:, :half], row[:, half:]))


def relative(neighbours_ref, a, k, first):
    return neighbours_ref[a, k] - (first + a) + REACH


def fold_kernel(tiles, half, neighbours_ref, valid_ref, pool_ref, cot_ref, up_ref, down_ref, acc):
    core = lax.axis_index("chan")
    first = lax.axis_index("tile") * tiles
    pool = pool_ref[...]
    for a in range(tiles):
        acc[...] = jnp.zeros_like(acc)
        for k in range(NEIGHBOURS):
            w = relative(neighbours_ref, a, k, first)
            piece = cot_ref[0, a, :, k * LEVELS : (k + 1) * LEVELS].astype(jnp.float32)
            acc[w, :, :LEVELS] += piece
        keep = valid_column(valid_ref, a, core, half)
        for w in range(SPAN):
            total = acc[w] * keep
            rounded = total.astype(jnp.bfloat16)
            up_ref[a, w] = rounded
            spread = jnp.dot(rounded[:, PIXELS:], pool, preferred_element_type=jnp.float32)
            down_ref[a, w] = (total[:, :PIXELS] + spread).astype(jnp.bfloat16)


def fold(neighbours, valid, pool, cotangent):
    tiles, half = cotangent.shape[1], cotangent.shape[2]
    return pl.pallas_call(
        functools.partial(fold_kernel, tiles, half),
        out_shape=(
            jax.ShapeDtypeStruct((tiles, SPAN, half, WIDE), jnp.bfloat16),
            jax.ShapeDtypeStruct((tiles, SPAN, half, PIXELS), jnp.bfloat16),
        ),
        in_specs=[SMEM, VMEM, VMEM, VMEM],
        out_specs=(VMEM, VMEM),
        scratch_shapes=[pltpu.VMEM((SPAN, half, WIDE), jnp.float32)],
        compiler_params=pltpu.CompilerParams(vmem_limit_bytes=24 * 2**20),
        cost_estimate=pl.CostEstimate(flops=2 * 10**8, bytes_accessed=4 * 10**6, transcendentals=0),
        name="fold",
    )(neighbours, valid, pool, cotangent)


def keys_kernel(tiles, half, x_ref, mine_ref, other_ref, own_ref, even_ref, odd_ref, window):
    core = lax.axis_index("chan")
    tile = lax.axis_index("tile")
    for a in range(tiles):
        here = x_ref[a, pl.ds(pl.multiple_of(core * half, half), half), :]
        there = x_ref[a, pl.ds(pl.multiple_of((1 - core) * half, half), half), :]
        turned = jnp.concatenate([here, there], axis=0).astype(jnp.float32).T.astype(jnp.bfloat16)
        for w in range(SPAN):
            grads = jnp.concatenate([mine_ref[a, w], other_ref[a, w]], axis=0)
            term = jnp.dot(turned, grads, preferred_element_type=jnp.float32)
            slot = a + w
            if a == 0 or w == SPAN - 1:
                window[slot] = term
            else:
                window[slot] += term
    own_ref[...] = window[tiles : 2 * tiles]
    parity = lax.rem(tile, 2)
    even = (1 - parity) * 2 * tiles
    odd = parity * 2 * tiles
    for a in range(tiles):
        even_ref[a] = window[even + a].astype(jnp.bfloat16)
        odd_ref[a] = window[odd + a].astype(jnp.bfloat16)


def keys(x, mine, other):
    tiles, pixels, channels = x.shape
    half = mine.shape[2]
    shape = (tiles, channels, pixels)
    return pl.pallas_call(
        functools.partial(keys_kernel, tiles, half),
        out_shape=(
            jax.ShapeDtypeStruct(shape, jnp.float32),
            jax.ShapeDtypeStruct(shape, jnp.bfloat16),
            jax.ShapeDtypeStruct(shape, jnp.bfloat16),
        ),
        in_specs=[VMEM] * 3,
        out_specs=(VMEM,) * 3,
        scratch_shapes=[pltpu.VMEM((3 * tiles, channels, pixels), jnp.float32)],
        compiler_params=pltpu.CompilerParams(vmem_limit_bytes=24 * 2**20),
        cost_estimate=pl.CostEstimate(flops=4 * 10**8, bytes_accessed=2 * 10**6, transcendentals=0),
        name="keys",
    )(x, mine, other)


def gate(pairing_ref, j, partners):
    if partners == 1:
        column = 1 - lax.axis_index("frame")
    else:
        column = j
    return pairing_ref[0, column].astype(jnp.float32) / 16.0


def returns_kernel(partners, pairing_ref, own_ref, even_ref, odd_ref, *out_refs):
    tile, count = lax.axis_index("tile"), lax.axis_size("tile")
    parity = lax.rem(tile, 2)
    has_even = jnp.logical_or(parity == 1, tile + 1 < count)
    has_odd = jnp.logical_or(jnp.logical_and(parity == 0, tile > 0), jnp.logical_and(parity == 1, tile + 1 < count))
    total = own_ref[...]
    total = total + jnp.where(has_even, even_ref[...].astype(jnp.float32), 0.0)
    total = total + jnp.where(has_odd, odd_ref[...].astype(jnp.float32), 0.0)
    for j in range(partners):
        out_refs[j][...] = (total * gate(pairing_ref, j, partners)).astype(jnp.bfloat16)


def returns(partners, pairing, own, even, odd):
    return pl.pallas_call(
        functools.partial(returns_kernel, partners),
        out_shape=(jax.ShapeDtypeStruct(own.shape, jnp.bfloat16),) * partners,
        in_specs=[SMEM] + [VMEM] * 3,
        out_specs=(VMEM,) * partners,
        cost_estimate=pl.CostEstimate(flops=10**5, bytes_accessed=5 * 10**5, transcendentals=0),
        name="returns",
    )(pairing, own, even, odd)


def scores_kernel(
    tiles, half, partners, neighbours_ref, pairing_ref, valid_ref, pool_ref, x_ref, xo_ref, up_ref, *refs
):
    inputs, (volume_ref, mine_ref, other_ref, pyramid, queries, table) = refs[: 6 * partners], refs[6 * partners :]
    core, tile = lax.axis_index("chan"), lax.axis_index("tile")
    first = tile * tiles
    parity = lax.rem(tile, 2)
    even = (1 - parity) * 2 * tiles
    odd = parity * 2 * tiles
    pool = pool_ref[...]
    rows = pl.ds(pl.multiple_of(core * half, half), half)
    channels = x_ref.shape[2]

    def both(mine, other):
        return jnp.concatenate([jnp.where(core == 0, mine, other), jnp.where(core == 0, other, mine)], axis=-1)

    for j in range(partners):
        group = inputs[6 * j : 6 * j + 6]
        for part, base in enumerate((tiles, even, odd)):
            for a in range(tiles):
                level = both(group[part][a], group[part + 3][a])
                coarse = jnp.dot(pool, level, preferred_element_type=jnp.float32)
                pyramid[j, base + a, :PIXELS] = level
                pyramid[j, base + a, PIXELS:] = coarse.astype(jnp.bfloat16)
    for a in range(tiles):
        keep = valid_column(valid_ref, a, core, half)
        row = both(x_ref[a, rows, :], xo_ref[a, rows, :]).astype(jnp.float32) * keep
        for j in range(partners):
            queries[j, a * half : (a + 1) * half] = (row * gate(pairing_ref, j, partners)).astype(jnp.bfloat16)
    for a in range(tiles):
        grad = jnp.zeros((half, 2 * channels), jnp.float32)
        for j in range(partners):
            term = jnp.zeros((half, 2 * channels), jnp.float32)
            for w in range(SPAN):
                term += jnp.dot(up_ref[a, w], pyramid[j, a + w], preferred_element_type=jnp.float32)
            grad += term * gate(pairing_ref, j, partners)
        low, high = grad[:, :channels], grad[:, channels:]
        mine_ref[a] = jnp.where(core == 0, low, high)
        other_ref[a] = jnp.where(core == 0, high, low).astype(jnp.bfloat16)
    for s in range(3 * tiles):
        total = jnp.zeros((tiles * half, WIDE), jnp.float32)
        for j in range(partners):
            total += lax.dot_general(
                queries[j], pyramid[j, s], (((1,), (1,)), ((), ())), preferred_element_type=jnp.float32
            )
        table[s] = total.astype(jnp.bfloat16)
    for a in range(tiles):
        for k in range(NEIGHBOURS):
            slot = relative(neighbours_ref, a, k, first) + a
            piece = table[slot, a * half : (a + 1) * half, :]
            volume_ref[0, a, :, k * LEVELS : (k + 1) * LEVELS] = piece[:, :LEVELS]


def scores(partners, neighbours, pairing, valid, pool, x, xo, up, windows):
    tiles, half = up.shape[0], up.shape[2]
    channels = x.shape[2]
    return pl.pallas_call(
        functools.partial(scores_kernel, tiles, half, partners),
        out_shape=(
            jax.ShapeDtypeStruct((1, tiles, half, NEIGHBOURS * LEVELS), jnp.bfloat16),
            jax.ShapeDtypeStruct((tiles, half, channels), jnp.float32),
            jax.ShapeDtypeStruct((tiles, half, channels), jnp.bfloat16),
        ),
        in_specs=[SMEM, SMEM] + [VMEM] * (5 + len(windows)),
        out_specs=(VMEM,) * 3,
        scratch_shapes=[
            pltpu.VMEM((partners, 3 * tiles, WIDE, 2 * channels), jnp.bfloat16),
            pltpu.VMEM((partners, tiles * half, 2 * channels), jnp.bfloat16),
            pltpu.VMEM((3 * tiles, tiles * half, WIDE), jnp.bfloat16),
        ],
        compiler_params=pltpu.CompilerParams(vmem_limit_bytes=32 * 2**20),
        cost_estimate=pl.CostEstimate(flops=10**9, bytes_accessed=4 * 10**6, transcendentals=0),
        name="scores",
    )(neighbours, pairing, valid, pool, x, xo, up, *windows)


def merge_kernel(tiles, half, partners, mine_ref, other_ref, *refs):
    keys_refs, out_ref = refs[:partners], refs[partners]
    core = lax.axis_index("chan")
    here = pl.ds(pl.multiple_of(core * half, half), half)
    there = pl.ds(pl.multiple_of((1 - core) * half, half), half)
    for a in range(tiles):
        total = keys_refs[0][a].astype(jnp.float32)
        for j in range(1, partners):
            total += keys_refs[j][a].astype(jnp.float32)
        out_ref[0, a] = total.T
        out_ref[0, a, here, :] += mine_ref[a]
        out_ref[0, a, there, :] += other_ref[a].astype(jnp.float32)


def merge(mine, other, returned):
    tiles, half, channels = mine.shape
    return pl.pallas_call(
        functools.partial(merge_kernel, tiles, half, len(returned)),
        out_shape=jax.ShapeDtypeStruct((1, tiles, 2 * half, channels), jnp.float32),
        in_specs=[VMEM] * (2 + len(returned)),
        out_specs=VMEM,
        cost_estimate=pl.CostEstimate(flops=10**5, bytes_accessed=7 * 10**5, transcendentals=0),
        name="merge",
    )(mine, other, *returned)


def local(features, neighbours, pairing, valid_tiles, cotangent):
    count = lax.axis_size("tile")
    cores = lax.axis_size("chan")
    links = frame_links(lax.axis_size("frame"))
    partners = len(links)
    pool = jnp.asarray(coarse_weights(), jnp.bfloat16)
    swap = [(c, (c + 1) % cores) for c in range(cores)]
    evens, odds = even_pairs(count), odd_pairs(count, cores)

    def over_even(z):
        return lax.ppermute(z, "tile", evens)

    def over_odd(z):
        return lax.ppermute(z, ("tile", "chan"), odds)

    def over_cores(z):
        return lax.ppermute(z, "chan", swap)

    x = features[0]
    arrived = [lax.ppermute(x, "frame", ahead) for ahead, _ in links]
    xo = over_cores(x)
    up, down = fold(neighbours, valid_tiles, pool, cotangent)
    down_other = over_cores(down)
    own, to_even, to_odd = keys(x, down, down_other)
    windows = []
    for y in arrived:
        parts = [y, over_even(y), over_odd(y)]
        windows += parts + [over_cores(z) for z in parts]
    sent = returns(partners, pairing, own, over_even(to_even), over_odd(to_odd))
    returned = [lax.ppermute(z, "frame", back) for z, (_, back) in zip(sent, links, strict=True)]
    volume, mine, other = scores(partners, neighbours, pairing, valid_tiles, pool, x, xo, up, windows)
    feature_grad = merge(mine, over_cores(other), returned)
    return volume, feature_grad


def solution(mesh):
    return jax.shard_map(
        local,
        mesh=mesh,
        in_specs=(
            P(("clip", "frame"), "tile", None, "chan"),
            P(("clip", "tile"), None),
            P(("clip", "frame"), None),
            P(("clip", "tile"), None),
            P(("clip", "frame"), "tile", "chan", None),
        ),
        out_specs=(
            P(("clip", "frame"), "tile", "chan", None),
            P(("clip", "frame"), "tile", None, "chan"),
        ),
        check_vma=False,
    )
```

```python
import functools

import jax
import jax.numpy as jnp
from jax import lax
from jax.experimental import pallas as pl
from jax.experimental.pallas import tpu as pltpu
from jax.sharding import PartitionSpec as P

CHANNELS = 256
SIDE = 16
PIXELS = 256
LEVELS = 340
NEIGHBOURS = 9
REACH = 2
SPAN = 2 * REACH + 1
COARSE = LEVELS - PIXELS
MARGIN = 16
PAD = 128
WIDE = PIXELS + PAD

VMEM = pl.BlockSpec(memory_space=pltpu.VMEM)
HBM = pl.BlockSpec(memory_space=pltpu.HBM)


def even_pairs(count):
    pairs = []
    for i in range(0, count - 1, 2):
        pairs += [(i, i + 1), (i + 1, i)]
    if count % 2:
        pairs.append((count - 1, count - 1))
    return pairs


def odd_pairs(count, cores):
    pairs, paired = [], set()
    for i in range(1, count - 1, 2):
        paired |= {i, i + 1}
        for c in range(cores):
            pairs += [(i * cores + c, (i + 1) * cores + c), ((i + 1) * cores + c, i * cores + c)]
    for i in range(count):
        if i not in paired:
            pairs += [(i * cores + c, i * cores + (c + 1) % cores) for c in range(cores)]
    return pairs


def frame_links(count):
    if count == 2:
        swap = [(0, 1), (1, 0)]
        return [(swap, swap)]
    onward = [(i, i + 1) for i in range(count - 1)]
    back = [(i + 1, i) for i in range(count - 1)]
    return [(onward, back), (back, onward)]


def coarse_weights(shape, pixel_axis):
    pixel = lax.broadcasted_iota(jnp.int32, shape, pixel_axis)
    cell = lax.broadcasted_iota(jnp.int32, shape, 1 - pixel_axis)
    row, column = lax.shift_right_logical(pixel, 4), jnp.bitwise_and(pixel, SIDE - 1)
    table = jnp.zeros(shape, jnp.float32)
    base = 0
    for level, across in ((1, 8), (2, 4), (3, 2)):
        target = base + lax.shift_right_logical(row, level) * across + lax.shift_right_logical(column, level)
        table = jnp.where(cell == target, 0.25**level, table)
        base += across * across
    return table.astype(jnp.bfloat16)


def column_of(row):
    n = row.shape[1]
    diagonal = lax.broadcasted_iota(jnp.int32, (n, n), 0) == lax.broadcasted_iota(jnp.int32, (n, n), 1)
    return jnp.sum(jnp.where(diagonal, row, 0.0), axis=1, keepdims=True)


def valid_row(valid_ref, a, core, half):
    row = valid_ref[a : a + 1, :].astype(jnp.float32)
    return jnp.where(core == 0, row[:, :half], row[:, half:])


def relative(neighbours_ref, a, k, first):
    return neighbours_ref[a, k] - (first + a) + REACH


def gate(pairing_ref, j, partners):
    if partners == 1:
        column = 1 - lax.axis_index("frame")
    else:
        column = j
    return pairing_ref[0, column].astype(jnp.float32) / 16.0


def entry_pairs(tiles):
    rows = LEVELS * tiles
    for k in range(0, NEIGHBOURS, 2):
        entries = range(k, min(k + 2, NEIGHBOURS))
        yield entries, k * rows, len(entries) * rows


def in_hbm(*arrays):
    return [pltpu.with_memory_space_constraint(z, pltpu.HBM) for z in arrays]


def copies(sources, targets, sems):
    started = [pltpu.make_async_copy(s, t, sems.at[i]) for i, (s, t) in enumerate(zip(sources, targets, strict=True))]
    for copy in started:
        copy.start()
    return started


def side_bases(tiles):
    parity = lax.rem(lax.axis_index("tile"), 2)
    return (1 - parity) * 2 * tiles, parity * 2 * tiles


def shape_of(shape, dtype=jnp.bfloat16):
    return jax.ShapeDtypeStruct(shape, dtype)


def call(kernel, name, outs, in_specs, out_specs, scratch, vmem_mib):
    return pl.pallas_call(
        kernel,
        out_shape=outs,
        in_specs=in_specs,
        out_specs=out_specs,
        scratch_shapes=scratch,
        compiler_params=pltpu.CompilerParams(vmem_limit_bytes=vmem_mib * 2**20),
        name=name,
    )


def fold_kernel(tiles, half, neighbours_hbm, valid_hbm, cot_hbm, features_hbm, down_ref, *refs):
    x_ref, neighbours_ref, valid_ref, cot_ref, stage, total, sems = refs
    core = lax.axis_index("chan")
    first = lax.axis_index("tile") * tiles
    parts = list(entry_pairs(tiles))
    views = [pl.ds(start, size) for _, start, size in parts]
    waits = copies(
        [neighbours_hbm, valid_hbm] + [cot_hbm.at[v] for v in views] + [features_hbm.at[0]],
        [neighbours_ref, valid_ref] + [cot_ref.at[v] for v in views] + [x_ref],
        sems,
    )
    pool = coarse_weights((PIXELS, PAD), 0)
    total[...] = jnp.zeros_like(total)
    waits[0].wait()
    waits[1].wait()
    for (entries, start, size), copy in zip(parts, waits[2 : 2 + len(parts)], strict=True):
        copy.wait()
        stage[:size] = cot_ref[start : start + size, :].astype(jnp.float32)
        for i, k in enumerate(entries):
            for a in range(tiles):
                w = relative(neighbours_ref, a, k, first)
                total[a, w, :LEVELS] += stage[pl.ds(i * LEVELS * tiles + a, LEVELS, stride=tiles), :]
    for a in range(tiles):
        keep = valid_row(valid_ref, a, core, half)
        for w in range(SPAN):
            coarse = total[a, w, PIXELS:].astype(jnp.bfloat16)
            spread = jnp.dot(pool, coarse, preferred_element_type=jnp.float32)
            down_ref[a, w] = ((total[a, w, :PIXELS] + spread) * keep).astype(jnp.bfloat16)
    waits[-1].wait()


def fold(neighbours, valid, cotangent, features):
    rows, half = cotangent.shape
    _, tiles, pixels, channels = features.shape
    return call(
        functools.partial(fold_kernel, tiles, half),
        "fold",
        (shape_of((tiles, SPAN, PIXELS, half)), shape_of((tiles, pixels, channels))),
        [HBM] * 4,
        (VMEM,) * 2,
        [
            pltpu.SMEM(neighbours.shape, jnp.int32),
            pltpu.VMEM(valid.shape, jnp.int32),
            pltpu.VMEM((rows, half), jnp.bfloat16),
            pltpu.VMEM((2 * LEVELS * tiles, half), jnp.float32),
            pltpu.VMEM((tiles, SPAN, WIDE, half), jnp.float32),
            pltpu.SemaphoreType.DMA((3 + (NEIGHBOURS + 1) // 2,)),
        ],
        8,
    )(*in_hbm(neighbours, valid, cotangent, features))


def halves(core, half):
    here = pl.ds(pl.multiple_of(core * half, half), half)
    there = pl.ds(pl.multiple_of((1 - core) * half, half), half)
    return here, there


def keys_kernel(tiles, half, x_ref, mine_ref, other_ref, own_ref, even_ref, odd_ref, window):
    here, there = halves(lax.axis_index("chan"), half)
    for a in range(tiles):
        queries = jnp.concatenate([x_ref[a, here, :], x_ref[a, there, :]], axis=0)
        for w in range(SPAN):
            grads = jnp.concatenate([mine_ref[a, w], other_ref[a, w]], axis=1)
            term = jnp.dot(grads, queries, preferred_element_type=jnp.float32)
            slot = a + w
            if a == 0 or w == SPAN - 1:
                window[slot] = term
            else:
                window[slot] += term
    own_ref[...] = window[tiles : 2 * tiles]
    even, odd = side_bases(tiles)
    for a in range(tiles):
        even_ref[a] = window[even + a].astype(jnp.bfloat16)
        odd_ref[a] = window[odd + a].astype(jnp.bfloat16)


def keys(x, mine, other):
    tiles, half = x.shape[0], mine.shape[3]
    return call(
        functools.partial(keys_kernel, tiles, half),
        "keys",
        (shape_of(x.shape, jnp.float32), shape_of(x.shape), shape_of(x.shape)),
        [VMEM] * 3,
        (VMEM,) * 3,
        [pltpu.VMEM((3 * tiles,) + x.shape[1:], jnp.float32)],
        6,
    )(x, mine, other)


def returns_kernel(partners, pairing_hbm, own_ref, even_ref, odd_ref, *refs):
    out_refs, (pairing_ref, sems) = refs[:partners], refs[partners:]
    (copy,) = copies([pairing_hbm], [pairing_ref], sems)
    tile, count = lax.axis_index("tile"), lax.axis_size("tile")
    parity = lax.rem(tile, 2)
    has_even = jnp.logical_or(parity == 1, tile + 1 < count)
    has_odd = jnp.logical_or(jnp.logical_and(parity == 0, tile > 0), jnp.logical_and(parity == 1, tile + 1 < count))
    total = own_ref[...]
    rows = own_ref.shape[0] * own_ref.shape[1]
    total = total + jnp.where(has_even, even_ref[...].astype(jnp.float32), 0.0)
    total = total + jnp.where(has_odd, odd_ref[...].astype(jnp.float32), 0.0)
    copy.wait()
    for j in range(partners):
        out_refs[j][:rows] = (total * gate(pairing_ref, j, partners)).astype(jnp.bfloat16).reshape(rows, -1)
        out_refs[j][rows:] = jnp.zeros_like(out_refs[j][rows:])


def returns(partners, pairing, own, even, odd):
    return call(
        functools.partial(returns_kernel, partners),
        "returns",
        (shape_of((own.shape[0] * own.shape[1] + MARGIN, own.shape[2])),) * partners,
        [HBM] + [VMEM] * 3,
        (VMEM,) * partners,
        [pltpu.SMEM(pairing.shape, jnp.int32), pltpu.SemaphoreType.DMA((1,))],
        3,
    )(*in_hbm(pairing), own, even, odd)


def join(mine, other):
    core = lax.axis_index("chan")
    return jnp.concatenate([jnp.where(core == 0, mine, other), jnp.where(core == 0, other, mine)], axis=-1)


def multiply(left, right, contract):
    return lax.dot_general(left, right, ((contract[:1], contract[1:]), ((), ())), preferred_element_type=jnp.float32)


def query_grads(mine_ref, other_ref, a, w, level):
    return multiply(jnp.concatenate([mine_ref[a, w], other_ref[a, w]], axis=1), level, (0, 0))


def near_kernel(tiles, half, partners, pairing_hbm, valid_hbm, down_ref, down_other_ref, *refs):
    (x_ref, xo_ref), same, rest = refs[:2], refs[2 : 2 + 2 * partners], refs[2 + 2 * partners :]
    queries_ref, fine_ref, coarse_ref, grad_ref, pairing_ref, valid_ref, sems = rest
    waits = copies([pairing_hbm, valid_hbm], [pairing_ref, valid_ref], sems)
    core = lax.axis_index("chan")
    pool = coarse_weights((PAD, PIXELS), 1)
    here, _ = halves(core, half)
    for copy in waits:
        copy.wait()
    for a in range(tiles):
        keep = column_of(valid_row(valid_ref, a, core, half))
        row = join(x_ref[a, here, :], xo_ref[a, here, :]).astype(jnp.float32) * keep
        for j in range(partners):
            queries_ref[j, a * half : (a + 1) * half] = (row * gate(pairing_ref, j, partners)).astype(jnp.bfloat16)
    grad = [None] * tiles
    for s in range(tiles):
        for j in range(partners):
            level_mine, level_other = same[2 * j][s], same[2 * j + 1][s]
            level = join(level_mine, level_other)
            coarse = jnp.dot(pool, level, preferred_element_type=jnp.float32).astype(jnp.bfloat16)
            fine_term = multiply(level, queries_ref[j], (1, 1))
            coarse_term = multiply(coarse, queries_ref[j], (1, 1))
            fine_ref[s] = fine_term if j == 0 else fine_ref[s] + fine_term
            coarse_ref[s] = coarse_term if j == 0 else coarse_ref[s] + coarse_term
            for a in range(tiles):
                term = query_grads(down_ref, down_other_ref, a, tiles + s - a, level_mine)
                term = term * gate(pairing_ref, j, partners)
                grad[a] = term if grad[a] is None else grad[a] + term
    for a in range(tiles):
        grad_ref[a] = grad[a]


def near(partners, pairing, valid, down, down_other, x, xo, same):
    tiles, half, channels = x.shape[0], down.shape[3], x.shape[2]
    both = 2 * channels
    return call(
        functools.partial(near_kernel, tiles, half, partners),
        "near",
        (
            shape_of((partners, tiles * half, both)),
            shape_of((tiles, PIXELS, tiles * half), jnp.float32),
            shape_of((tiles, PAD, tiles * half), jnp.float32),
            shape_of((tiles, 2 * half, channels), jnp.float32),
        ),
        [HBM, HBM] + [VMEM] * (4 + len(same)),
        (VMEM,) * 4,
        [
            pltpu.SMEM(pairing.shape, jnp.int32),
            pltpu.VMEM(valid.shape, jnp.int32),
            pltpu.SemaphoreType.DMA((2,)),
        ],
        8,
    )(*in_hbm(pairing, valid), down, down_other, x, xo, *same)


def side_order(tiles):
    parity = lax.rem(lax.axis_index("tile"), 2)
    return (1 - parity) * tiles, parity * tiles


def sides_kernel(tiles, half, partners, pairing_hbm, down_ref, down_other_ref, near_ref, *refs):
    inputs, (grad_ref, levels, pairing_ref, sems) = refs[: 2 * partners], refs[2 * partners :]
    (copy,) = copies([pairing_hbm], [pairing_ref], sems)
    here, there = halves(lax.axis_index("chan"), half)
    even, odd = side_order(tiles)
    for j in range(partners):
        levels[j, pl.ds(even, tiles)] = inputs[2 * j][...]
        levels[j, pl.ds(odd, tiles)] = inputs[2 * j + 1][...]
    copy.wait()
    for a in range(tiles):
        grad = near_ref[a]
        for j in range(partners):
            term = None
            for w in range(SPAN):
                slot = a + w
                if tiles <= slot < 2 * tiles:
                    continue
                part = query_grads(down_ref, down_other_ref, a, w, levels[j, slot if slot < tiles else slot - tiles])
                term = part if term is None else term + part
            grad = grad + term * gate(pairing_ref, j, partners)
        grad_ref[a, here, :] = grad[:half]
        grad_ref[a, there, :] = grad[half:]


def sides(partners, pairing, down, down_other, near_grad, beside):
    tiles, rows, channels = near_grad.shape
    return call(
        functools.partial(sides_kernel, tiles, rows // 2, partners),
        "sides",
        shape_of(near_grad.shape, jnp.float32),
        [HBM] + [VMEM] * (3 + len(beside)),
        VMEM,
        [
            pltpu.VMEM((partners, 2 * tiles, PIXELS, channels), jnp.bfloat16),
            pltpu.SMEM(pairing.shape, jnp.int32),
            pltpu.SemaphoreType.DMA((1,)),
        ],
        6,
    )(*in_hbm(pairing), down, down_other, near_grad, *beside)


def volume_kernel(tiles, half, partners, neighbours_hbm, queries_ref, near_fine, near_coarse, *refs):
    inputs, rest = refs[: 4 * partners], refs[4 * partners :]
    volume_hbm, neighbours_ref, fine_table, coarse_table, stage, volume_ref, sems = rest
    (neighbours_copy,) = copies([neighbours_hbm], [neighbours_ref], sems)
    first = lax.axis_index("tile") * tiles
    pool = coarse_weights((PAD, PIXELS), 1)
    fine_table[tiles : 2 * tiles] = near_fine[...]
    coarse_table[tiles : 2 * tiles] = near_coarse[...]
    for part, base in enumerate(side_bases(tiles)):
        for a in range(tiles):
            fine, coarse = None, None
            for j in range(partners):
                level = join(inputs[4 * j + part][a], inputs[4 * j + 2 + part][a])
                cells = jnp.dot(pool, level, preferred_element_type=jnp.float32).astype(jnp.bfloat16)
                fine_term = multiply(level, queries_ref[j], (1, 1))
                coarse_term = multiply(cells, queries_ref[j], (1, 1))
                fine = fine_term if fine is None else fine + fine_term
                coarse = coarse_term if coarse is None else coarse + coarse_term
            fine_table[base + a] = fine
            coarse_table[base + a] = coarse
    neighbours_copy.wait()
    waits = []
    for i_part, (entries, start, size) in enumerate(entry_pairs(tiles)):
        for i, k in enumerate(entries):
            for a in range(tiles):
                slot = relative(neighbours_ref, a, k, first) + a
                lanes = slice(a * half, (a + 1) * half)
                base = i * LEVELS * tiles + a
                stage[pl.ds(base, PIXELS, stride=tiles), :] = fine_table[slot, :, lanes]
                stage[pl.ds(base + PIXELS * tiles, COARSE, stride=tiles), :] = coarse_table[slot, :COARSE, lanes]
        rows = pl.ds(start, size)
        volume_ref[rows, :] = stage[:size].astype(jnp.bfloat16)
        copy = pltpu.make_async_copy(volume_ref.at[rows], volume_hbm.at[rows], sems.at[1 + i_part])
        copy.start()
        waits.append(copy)
    for copy in waits:
        copy.wait()


def volumes(partners, neighbours, queries, near_fine, near_coarse, beside):
    tiles, half = near_fine.shape[0], near_fine.shape[2] // near_fine.shape[0]
    rows = NEIGHBOURS * LEVELS * tiles
    return call(
        functools.partial(volume_kernel, tiles, half, partners),
        "volume",
        shape_of((rows, half)),
        [HBM] + [VMEM] * (3 + len(beside)),
        HBM,
        [
            pltpu.SMEM(neighbours.shape, jnp.int32),
            pltpu.VMEM((3 * tiles, PIXELS, tiles * half), jnp.float32),
            pltpu.VMEM((3 * tiles, PAD, tiles * half), jnp.float32),
            pltpu.VMEM((2 * LEVELS * tiles, half), jnp.float32),
            pltpu.VMEM((rows, half), jnp.bfloat16),
            pltpu.SemaphoreType.DMA((1 + (NEIGHBOURS + 1) // 2,)),
        ],
        12,
    )(*in_hbm(neighbours), queries, near_fine, near_coarse, *beside)


def merge_kernel(partners, grad_ref, *refs):
    total = grad_ref[...]
    for j in range(partners):
        total = total + refs[j][: total.shape[0] * total.shape[1]].astype(jnp.float32).reshape(total.shape)
    refs[partners][0] = total


def merge(grad, returned):
    return call(
        functools.partial(merge_kernel, len(returned)),
        "merge",
        shape_of((1,) + grad.shape, jnp.float32),
        [VMEM] * (1 + len(returned)),
        VMEM,
        [],
        2,
    )(grad, *returned)


def after(value, earlier):
    return lax.optimization_barrier((value, earlier))[0]


def local(features, neighbours, pairing, valid_tiles, cotangent):
    count = lax.axis_size("tile")
    cores = lax.axis_size("chan")
    links = frame_links(lax.axis_size("frame"))
    partners = len(links)
    tiles, half = cotangent.shape[1:3]
    swap = [(c, (c + 1) % cores) for c in range(cores)]
    evens, odds = even_pairs(count), odd_pairs(count, cores)

    def over_even(z):
        return lax.ppermute(z, "tile", evens)

    def over_odd(z):
        return lax.ppermute(z, ("tile", "chan"), odds)

    def over_cores(z):
        return lax.ppermute(z, "chan", swap)

    upstream = jnp.transpose(cotangent[0], (2, 0, 1)).reshape(NEIGHBOURS * LEVELS * tiles, half)
    down, x = fold(neighbours, valid_tiles, upstream, features)
    down_other = over_cores(down)
    arrived = [lax.ppermute(x, "frame", ahead) for ahead, _ in links]
    xo = over_cores(x)
    own, to_even, to_odd = keys(x, down, down_other)
    arrived = [after(y, own) for y in arrived]
    beside = [(over_even(y), over_odd(y)) for y in arrived]
    sent = returns(partners, pairing, own, over_even(to_even), over_odd(to_odd))
    returned = [lax.ppermute(z, "frame", back) for z, (_, back) in zip(sent, links, strict=True)]
    same = []
    for y in arrived:
        same += [after(y, sent[0]), after(over_cores(y), sent[0])]
    queries, near_fine, near_coarse, near_grad = near(partners, pairing, valid_tiles, down, down_other, x, xo, same)
    mine, exchanged = [], []
    for even, odd in beside:
        even = after(even, near_grad)
        odd = after(odd, even)
        mine += [even, odd]
        exchanged += [even, odd, over_cores(even), over_cores(odd)]
    grad = sides(partners, pairing, down, down_other, near_grad, mine)
    exchanged = [after(z, grad) for z in exchanged]
    volume = volumes(partners, neighbours, queries, near_fine, near_coarse, exchanged)
    feature_grad = merge(grad, returned)
    volume = jnp.transpose(volume.reshape(NEIGHBOURS * LEVELS, tiles, half), (1, 2, 0))
    return volume[None], feature_grad


def solution(mesh):
    return jax.shard_map(
        local,
        mesh=mesh,
        in_specs=(
            P(("clip", "frame"), "tile", None, "chan"),
            P(("clip", "tile"), None),
            P(("clip", "frame"), None),
            P(("clip", "tile"), None),
            P(("clip", "frame"), "tile", "chan", None),
        ),
        out_specs=(
            P(("clip", "frame"), "tile", "chan", None),
            P(("clip", "frame"), "tile", None, "chan"),
        ),
        check_vma=False,
    )
```

```python
import functools

import jax
import jax.numpy as jnp
from jax import lax
from jax.experimental import pallas as pl
from jax.experimental.pallas import tpu as pltpu
from jax.sharding import PartitionSpec as P

CHANNELS = 256
SIDE = 16
PIXELS = 256
LEVELS = 340
NEIGHBOURS = 9
REACH = 2
SPAN = 2 * REACH + 1
COARSE = LEVELS - PIXELS
MARGIN = 16
PAD = 128
WIDE = PIXELS + PAD

VMEM = pl.BlockSpec(memory_space=pltpu.VMEM)
HBM = pl.BlockSpec(memory_space=pltpu.HBM)


def even_pairs(count):
    pairs = []
    for i in range(0, count - 1, 2):
        pairs += [(i, i + 1), (i + 1, i)]
    if count % 2:
        pairs.append((count - 1, count - 1))
    return pairs


def odd_pairs(count, cores):
    pairs, paired = [], set()
    for i in range(1, count - 1, 2):
        paired |= {i, i + 1}
        for c in range(cores):
            pairs += [(i * cores + c, (i + 1) * cores + c), ((i + 1) * cores + c, i * cores + c)]
    for i in range(count):
        if i not in paired:
            pairs += [(i * cores + c, i * cores + (c + 1) % cores) for c in range(cores)]
    return pairs


def frame_links(count):
    if count == 2:
        swap = [(0, 1), (1, 0)]
        return [(swap, swap)]
    onward = [(i, i + 1) for i in range(count - 1)]
    back = [(i + 1, i) for i in range(count - 1)]
    return [(onward, back), (back, onward)]


def coarse_weights(shape, pixel_axis):
    pixel = lax.broadcasted_iota(jnp.int32, shape, pixel_axis)
    cell = lax.broadcasted_iota(jnp.int32, shape, 1 - pixel_axis)
    row, column = lax.shift_right_logical(pixel, 4), jnp.bitwise_and(pixel, SIDE - 1)
    table = jnp.zeros(shape, jnp.float32)
    base = 0
    for level, across in ((1, 8), (2, 4), (3, 2)):
        target = base + lax.shift_right_logical(row, level) * across + lax.shift_right_logical(column, level)
        table = jnp.where(cell == target, 0.25**level, table)
        base += across * across
    return table.astype(jnp.bfloat16)


def column_of(row):
    n = row.shape[1]
    diagonal = lax.broadcasted_iota(jnp.int32, (n, n), 0) == lax.broadcasted_iota(jnp.int32, (n, n), 1)
    return jnp.sum(jnp.where(diagonal, row, 0.0), axis=1, keepdims=True)


def valid_row(valid_ref, a, core, half):
    row = valid_ref[a : a + 1, :].astype(jnp.float32)
    return jnp.where(core == 0, row[:, :half], row[:, half:])


def relative(neighbours_ref, a, k, first):
    return neighbours_ref[a, k] - (first + a) + REACH


def gate(pairing_ref, j, partners):
    if partners == 1:
        column = 1 - lax.axis_index("frame")
    else:
        column = j
    return pairing_ref[0, column].astype(jnp.float32) / 16.0


def entry_pairs(tiles):
    rows = LEVELS * tiles
    for k in range(0, NEIGHBOURS, 2):
        entries = range(k, min(k + 2, NEIGHBOURS))
        yield entries, k * rows, len(entries) * rows


def in_hbm(*arrays):
    return [pltpu.with_memory_space_constraint(z, pltpu.HBM) for z in arrays]


def copies(sources, targets, sems):
    started = [pltpu.make_async_copy(s, t, sems.at[i]) for i, (s, t) in enumerate(zip(sources, targets, strict=True))]
    for copy in started:
        copy.start()
    return started


def side_bases(tiles):
    parity = lax.rem(lax.axis_index("tile"), 2)
    return (1 - parity) * 2 * tiles, parity * 2 * tiles


def shape_of(shape, dtype=jnp.bfloat16):
    return jax.ShapeDtypeStruct(shape, dtype)


def call(kernel, name, outs, in_specs, out_specs, scratch, vmem_mib):
    return pl.pallas_call(
        kernel,
        out_shape=outs,
        in_specs=in_specs,
        out_specs=out_specs,
        scratch_shapes=scratch,
        compiler_params=pltpu.CompilerParams(vmem_limit_bytes=vmem_mib * 2**20),
        name=name,
    )


def fold_kernel(tiles, half, partners, neighbours_hbm, valid_hbm, pairing_hbm, cot_hbm, features_hbm, *refs):
    folded_ref, x_ref, gates_ref, keep_ref, pool_ref, list_ref = refs[:6]
    neighbours_ref, valid_ref, pairing_ref, cot_ref, stage, total, sems = refs[6:]
    core = lax.axis_index("chan")
    first = lax.axis_index("tile") * tiles
    parts = list(entry_pairs(tiles))
    views = [pl.ds(start, size) for _, start, size in parts]
    small, (features_copy, list_copy, *waits) = split(
        copies(
            [neighbours_hbm, valid_hbm, pairing_hbm, features_hbm.at[0], neighbours_hbm] + [cot_hbm.at[v] for v in views],
            [neighbours_ref, valid_ref, pairing_ref, x_ref, list_ref] + [cot_ref.at[v] for v in views],
            sems,
        ),
        3,
    )
    pool_ref[...] = coarse_weights((PAD, PIXELS), 1)
    pool = coarse_weights((PIXELS, PAD), 0)
    total[...] = jnp.zeros_like(total)
    for copy in small:
        copy.wait()
    keep = [valid_row(valid_ref, a, core, half) for a in range(tiles)]
    columns = [jnp.broadcast_to(column_of(row), (half, half)) for row in keep]
    for j in range(partners):
        weight = gate(pairing_ref, j, partners)
        gates_ref[j] = jnp.full(gates_ref.shape[1:], weight, jnp.float32)
        for a in range(tiles):
            keep_ref[j, a * half : (a + 1) * half] = columns[a] * weight
    for (entries, start, size), copy in zip(parts, waits, strict=True):
        copy.wait()
        stage[:size] = cot_ref[start : start + size, :].astype(jnp.float32)
        for i, k in enumerate(entries):
            for a in range(tiles):
                w = relative(neighbours_ref, a, k, first)
                total[a, w, :LEVELS] += stage[pl.ds(i * LEVELS * tiles + a, LEVELS, stride=tiles), :]
    for a in range(tiles):
        for w in range(SPAN):
            coarse = total[a, w, PIXELS:].astype(jnp.bfloat16)
            spread = jnp.dot(pool, coarse, preferred_element_type=jnp.float32)
            folded_ref[fold_rows(a, w)] = ((total[a, w, :PIXELS] + spread) * keep[a]).astype(jnp.bfloat16)
    features_copy.wait()
    list_copy.wait()
    _, there = halves(core, half)
    for a in range(tiles):
        folded_ref[query_rows(tiles, half, a)] = x_ref[a, there, :]


def split(items, count):
    return items[:count], items[count:]


def fold_rows(a, w):
    start = (a * SPAN + w) * PIXELS
    return slice(start, start + PIXELS)


def query_rows(tiles, half, a):
    start = tiles * SPAN * PIXELS + a * half
    return slice(start, start + half)


def fold(partners, neighbours, valid, pairing, cotangent, features):
    rows, half = cotangent.shape
    _, tiles, pixels, channels = features.shape
    return call(
        functools.partial(fold_kernel, tiles, half, partners),
        "fold",
        (
            shape_of((tiles * SPAN * PIXELS + tiles * half, half)),
            shape_of((tiles, pixels, channels)),
            shape_of((partners, 8, channels), jnp.float32),
            shape_of((partners, tiles * half, channels), jnp.float32),
            shape_of((PAD, PIXELS)),
            shape_of(neighbours.shape, jnp.int32),
        ),
        [HBM] * 5,
        (VMEM,) * 6,
        [
            pltpu.SMEM(neighbours.shape, jnp.int32),
            pltpu.VMEM(valid.shape, jnp.int32),
            pltpu.SMEM(pairing.shape, jnp.int32),
            pltpu.VMEM((rows, half), jnp.bfloat16),
            pltpu.VMEM((2 * LEVELS * tiles, half), jnp.float32),
            pltpu.VMEM((tiles, SPAN, WIDE, half), jnp.float32),
            pltpu.SemaphoreType.DMA((5 + (NEIGHBOURS + 1) // 2,)),
        ],
        8,
    )(*in_hbm(neighbours, valid, pairing, cotangent, features))


def halves(core, half):
    here = pl.ds(pl.multiple_of(core * half, half), half)
    there = pl.ds(pl.multiple_of((1 - core) * half, half), half)
    return here, there


def keys_kernel(tiles, half, x_ref, mine_ref, other_ref, own_ref, even_ref, odd_ref, window):
    here, there = halves(lax.axis_index("chan"), half)
    for a in range(tiles):
        queries = jnp.concatenate([x_ref[a, here, :], x_ref[a, there, :]], axis=0)
        for w in range(SPAN):
            grads = jnp.concatenate([mine_ref[fold_rows(a, w)], other_ref[fold_rows(a, w)]], axis=1)
            term = jnp.dot(grads, queries, preferred_element_type=jnp.float32)
            slot = a + w
            if a == 0 or w == SPAN - 1:
                window[slot] = term
            else:
                window[slot] += term
    own_ref[...] = window[tiles : 2 * tiles]
    even, odd = side_bases(tiles)
    for a in range(tiles):
        even_ref[a] = window[even + a].astype(jnp.bfloat16)
        odd_ref[a] = window[odd + a].astype(jnp.bfloat16)


def keys(x, mine, other):
    tiles, half = x.shape[0], mine.shape[1]
    return call(
        functools.partial(keys_kernel, tiles, half),
        "keys",
        (shape_of(x.shape, jnp.float32), shape_of(x.shape), shape_of(x.shape)),
        [VMEM] * 3,
        (VMEM,) * 3,
        [pltpu.VMEM((3 * tiles,) + x.shape[1:], jnp.float32)],
        6,
    )(x, mine, other)


def returns_kernel(partners, gates_ref, own_ref, even_ref, odd_ref, *out_refs):
    tile, count = lax.axis_index("tile"), lax.axis_size("tile")
    parity = lax.rem(tile, 2)
    has_even = jnp.logical_or(parity == 1, tile + 1 < count)
    has_odd = jnp.logical_or(jnp.logical_and(parity == 0, tile > 0), jnp.logical_and(parity == 1, tile + 1 < count))
    tiles, pixels, _ = own_ref.shape
    for a in range(tiles):
        total = own_ref[a]
        total = total + jnp.where(has_even, even_ref[a].astype(jnp.float32), 0.0)
        total = total + jnp.where(has_odd, odd_ref[a].astype(jnp.float32), 0.0)
        for j in range(partners):
            out_refs[j][a * pixels : (a + 1) * pixels] = (total * gates_ref[j, :1]).astype(jnp.bfloat16)
    for j in range(partners):
        out_refs[j][tiles * pixels :] = jnp.zeros((MARGIN, out_refs[j].shape[1]), jnp.bfloat16)


def returns(partners, gates, own, even, odd):
    tiles, pixels, channels = own.shape
    return call(
        functools.partial(returns_kernel, partners),
        "returns",
        (shape_of((tiles * pixels + MARGIN, channels)),) * partners,
        [VMEM] * 4,
        (VMEM,) * partners,
        [],
        3,
    )(gates, own, even, odd)


def join(mine, other):
    core = lax.axis_index("chan")
    return jnp.concatenate([jnp.where(core == 0, mine, other), jnp.where(core == 0, other, mine)], axis=-1)


def multiply(left, right, contract):
    return lax.dot_general(left, right, ((contract[:1], contract[1:]), ((), ())), preferred_element_type=jnp.float32)


def window_slots(tiles):
    even, odd = side_bases(tiles)
    return tiles, even, odd


def sides_kernel(tiles, half, partners, gates_ref, folded_ref, other_ref, *refs):
    inputs, (grad_ref, levels) = refs[: 3 * partners], refs[3 * partners :]
    here, there = halves(lax.axis_index("chan"), half)
    for j in range(partners):
        for part, base in enumerate(window_slots(tiles)):
            levels[j, pl.ds(base, tiles)] = inputs[3 * j + part][...]
    for a in range(tiles):
        grad = None
        for j in range(partners):
            term = None
            for w in range(SPAN):
                both = jnp.concatenate([folded_ref[fold_rows(a, w)], other_ref[fold_rows(a, w)]], axis=1)
                part = multiply(both, levels[j, a + w], (0, 0))
                term = part if term is None else term + part
            term = term * gates_ref[j, :1]
            grad = term if grad is None else grad + term
        grad_ref[a, here, :] = grad[:half]
        grad_ref[a, there, :] = grad[half:]


def sides(partners, gates, folded, other, windows):
    tiles, pixels, channels = windows[0].shape
    return call(
        functools.partial(sides_kernel, tiles, pixels // 2, partners),
        "sides",
        shape_of(windows[0].shape, jnp.float32),
        [VMEM] * (3 + len(windows)),
        VMEM,
        [pltpu.VMEM((partners, 3 * tiles, pixels, channels), jnp.bfloat16)],
        6,
    )(gates, folded, other, *windows)


def near_kernel(tiles, half, partners, keep_ref, pool_ref, x_ref, other_ref, *refs):
    same, (queries_ref, fine_ref, coarse_ref) = refs[: 2 * partners], refs[2 * partners :]
    here, _ = halves(lax.axis_index("chan"), half)
    mine = jnp.concatenate([x_ref[a, here, :] for a in range(tiles)], axis=0).astype(jnp.float32)
    other = jnp.concatenate([other_ref[query_rows(tiles, half, a)] for a in range(tiles)], axis=0).astype(jnp.float32)
    pool = pool_ref[...]
    for j in range(partners):
        queries_ref[j] = join(mine * keep_ref[j], other * keep_ref[j]).T.astype(jnp.bfloat16)
    for s in range(tiles):
        fine, coarse = None, None
        for j in range(partners):
            level = join(same[2 * j][s], same[2 * j + 1][s])
            cells = jnp.dot(pool, level, preferred_element_type=jnp.float32).astype(jnp.bfloat16)
            fine_term = multiply(level, queries_ref[j], (1, 0))
            coarse_term = multiply(cells, queries_ref[j], (1, 0))
            fine = fine_term if fine is None else fine + fine_term
            coarse = coarse_term if coarse is None else coarse + coarse_term
        fine_ref[s] = fine
        coarse_ref[s] = coarse


def near(partners, keep, pool, x, other, same):
    tiles, pixels, channels = x.shape
    return call(
        functools.partial(near_kernel, tiles, pixels // 2, partners),
        "near",
        (
            shape_of((partners, 2 * channels, tiles * pixels // 2)),
            shape_of((tiles, pixels, tiles * pixels // 2), jnp.float32),
            shape_of((tiles, PAD, tiles * pixels // 2), jnp.float32),
        ),
        [VMEM] * (4 + len(same)),
        (VMEM,) * 3,
        [],
        6,
    )(keep, pool, x, other, *same)


def volume_kernel(tiles, half, partners, list_ref, queries_ref, near_fine, near_coarse, pool_ref, part_ref, *refs):
    inputs, returned, rest = refs[: 4 * partners], refs[4 * partners : 5 * partners], refs[5 * partners :]
    volume_hbm, grad_hbm, neighbours_ref, levels, cells, fine_table, coarse_table = rest[:7]
    stage, volume_ref, grad_ref, sems = rest[7:]
    (neighbours_copy,) = copies([list_ref], [neighbours_ref], sems)
    first = lax.axis_index("tile") * tiles
    pixels = grad_ref.shape[1]
    for a in range(tiles):
        total = part_ref[a]
        for j in range(partners):
            total = total + returned[j][a * pixels : (a + 1) * pixels].astype(jnp.float32)
        grad_ref[a] = total
    waits = [pltpu.make_async_copy(grad_ref, grad_hbm.at[0], sems.at[1])]
    waits[0].start()
    pool = pool_ref[...]
    for j in range(partners):
        for part in range(2):
            for a in range(tiles):
                level = join(inputs[4 * j + part][a], inputs[4 * j + 2 + part][a])
                at = part * tiles + a
                levels[j, at * PIXELS : (at + 1) * PIXELS] = level
                cells[j, at * PAD : (at + 1) * PAD] = jnp.dot(
                    pool, level, preferred_element_type=jnp.float32
                ).astype(jnp.bfloat16)
    fine_table[tiles : 2 * tiles] = near_fine[...]
    coarse_table[tiles : 2 * tiles] = near_coarse[...]
    for keys_at, table in ((levels, fine_table), (cells, coarse_table)):
        total = multiply(keys_at[0], queries_ref[0], (1, 0))
        for j in range(1, partners):
            total = total + multiply(keys_at[j], queries_ref[j], (1, 0))
        total = total.reshape(2, tiles, table.shape[1], tiles * half)
        for part, base in enumerate(side_bases(tiles)):
            table[pl.ds(base, tiles)] = total[part]
    neighbours_copy.wait()
    for i_part, (entries, start, size) in enumerate(entry_pairs(tiles)):
        for i, k in enumerate(entries):
            for a in range(tiles):
                slot = relative(neighbours_ref, a, k, first) + a
                lanes = slice(a * half, (a + 1) * half)
                base = i * LEVELS * tiles + a
                stage[pl.ds(base, PIXELS, stride=tiles), :] = fine_table[slot, :, lanes]
                stage[pl.ds(base + PIXELS * tiles, COARSE, stride=tiles), :] = coarse_table[slot, :COARSE, lanes]
        rows = pl.ds(start, size)
        volume_ref[rows, :] = stage[:size].astype(jnp.bfloat16)
        copy = pltpu.make_async_copy(volume_ref.at[rows], volume_hbm.at[rows], sems.at[2 + i_part])
        copy.start()
        waits.append(copy)
    for copy in waits:
        copy.wait()


def volumes(partners, neighbours, queries, near_fine, near_coarse, pool, grad, beside, returned):
    tiles, pixels, channels = grad.shape
    half = pixels // 2
    rows = NEIGHBOURS * LEVELS * tiles
    return call(
        functools.partial(volume_kernel, tiles, half, partners),
        "volume",
        (shape_of((rows, half)), shape_of((1,) + grad.shape, jnp.float32)),
        [VMEM] * (6 + len(beside) + len(returned)),
        (HBM, HBM),
        [
            pltpu.SMEM(neighbours.shape, jnp.int32),
            pltpu.VMEM((partners, 2 * tiles * PIXELS, 2 * channels), jnp.bfloat16),
            pltpu.VMEM((partners, 2 * tiles * PAD, 2 * channels), jnp.bfloat16),
            pltpu.VMEM((3 * tiles, PIXELS, tiles * half), jnp.float32),
            pltpu.VMEM((3 * tiles, PAD, tiles * half), jnp.float32),
            pltpu.VMEM((2 * LEVELS * tiles, half), jnp.float32),
            pltpu.VMEM((rows, half), jnp.bfloat16),
            pltpu.VMEM(grad.shape, jnp.float32),
            pltpu.SemaphoreType.DMA((2 + (NEIGHBOURS + 1) // 2,)),
        ],
        12,
    )(neighbours, queries, near_fine, near_coarse, pool, grad, *beside, *returned)


def after(value, earlier):
    return lax.optimization_barrier((value, earlier))[0]


def local(features, neighbours, pairing, valid_tiles, cotangent):
    count = lax.axis_size("tile")
    cores = lax.axis_size("chan")
    links = frame_links(lax.axis_size("frame"))
    partners = len(links)
    tiles, half = cotangent.shape[1:3]
    swap = [(c, (c + 1) % cores) for c in range(cores)]
    evens, odds = even_pairs(count), odd_pairs(count, cores)

    def over_even(z):
        return lax.ppermute(z, "tile", evens)

    def over_odd(z):
        return lax.ppermute(z, ("tile", "chan"), odds)

    def over_cores(z):
        return lax.ppermute(z, "chan", swap)

    upstream = jnp.transpose(cotangent[0], (2, 0, 1)).reshape(NEIGHBOURS * LEVELS * tiles, half)
    folded, x, gates, keep, pool, listed = fold(partners, neighbours, valid_tiles, pairing, upstream, features)
    other = over_cores(folded)
    arrived = [lax.ppermute(x, "frame", ahead) for ahead, _ in links]
    own, to_even, to_odd = keys(x, folded, other)
    arrived = [after(y, own) for y in arrived]
    beside = [(over_even(y), over_odd(y)) for y in arrived]
    from_odd = over_odd(to_odd)
    from_even = after(over_even(to_even), from_odd)
    sent = returns(partners, gates, own, from_even, from_odd)
    returned = [lax.ppermute(z, "frame", back) for z, (_, back) in zip(sent, links, strict=True)]
    same = []
    for y in arrived:
        same += [after(y, sent[0]), after(over_cores(y), sent[0])]
    queries, near_fine, near_coarse = near(partners, keep, pool, x, other, same)
    mine, exchanged = [], []
    for y, (even, odd) in zip(arrived, beside, strict=True):
        even = after(even, near_fine)
        odd = after(odd, even)
        mine += [y, even, odd]
        exchanged += [even, odd, over_cores(even), over_cores(odd)]
    grad = sides(partners, gates, folded, other, mine)
    exchanged = [after(z, grad) for z in exchanged]
    volume, feature_grad = volumes(
        partners, listed, queries, near_fine, near_coarse, pool, grad, exchanged, returned
    )
    volume = jnp.transpose(volume.reshape(NEIGHBOURS * LEVELS, tiles, half), (1, 2, 0))
    return volume[None], feature_grad


def solution(mesh):
    return jax.shard_map(
        local,
        mesh=mesh,
        in_specs=(
            P(("clip", "frame"), "tile", None, "chan"),
            P(("clip", "tile"), None),
            P(("clip", "frame"), None),
            P(("clip", "tile"), None),
            P(("clip", "frame"), "tile", "chan", None),
        ),
        out_specs=(
            P(("clip", "frame"), "tile", "chan", None),
            P(("clip", "frame"), "tile", None, "chan"),
        ),
        check_vma=False,
    )
```

```python
import functools

import jax
import jax.numpy as jnp
from jax import lax
from jax.experimental import pallas as pl
from jax.experimental.pallas import tpu as pltpu
from jax.sharding import PartitionSpec as P

CHANNELS = 256
SIDE = 16
PIXELS = 256
LEVELS = 340
NEIGHBOURS = 9
REACH = 2
SPAN = 2 * REACH + 1
COARSE = LEVELS - PIXELS
MARGIN = 16
STAGES = 9
PAD = 128
WIDE = PIXELS + PAD

VMEM = pl.BlockSpec(memory_space=pltpu.VMEM)
HBM = pl.BlockSpec(memory_space=pltpu.HBM)


def even_pairs(count):
    pairs = []
    for i in range(0, count - 1, 2):
        pairs += [(i, i + 1), (i + 1, i)]
    if count % 2:
        pairs.append((count - 1, count - 1))
    return pairs


def odd_pairs(count, cores):
    pairs, paired = [], set()
    for i in range(1, count - 1, 2):
        paired |= {i, i + 1}
        for c in range(cores):
            pairs += [(i * cores + c, (i + 1) * cores + c), ((i + 1) * cores + c, i * cores + c)]
    for i in range(count):
        if i not in paired:
            pairs += [(i * cores + c, i * cores + (c + 1) % cores) for c in range(cores)]
    return pairs


def frame_links(count):
    if count == 2:
        swap = [(0, 1), (1, 0)]
        return [(swap, swap)]
    onward = [(i, i + 1) for i in range(count - 1)]
    back = [(i + 1, i) for i in range(count - 1)]
    return [(onward, back), (back, onward)]


def coarse_weights(shape, pixel_axis):
    pixel = lax.broadcasted_iota(jnp.int32, shape, pixel_axis)
    cell = lax.broadcasted_iota(jnp.int32, shape, 1 - pixel_axis)
    row, column = lax.shift_right_logical(pixel, 4), jnp.bitwise_and(pixel, SIDE - 1)
    table = jnp.zeros(shape, jnp.float32)
    base = 0
    for level, across in ((1, 8), (2, 4), (3, 2)):
        target = base + lax.shift_right_logical(row, level) * across + lax.shift_right_logical(column, level)
        table = jnp.where(cell == target, 0.25**level, table)
        base += across * across
    return table.astype(jnp.bfloat16)


def column_of(row):
    n = row.shape[1]
    diagonal = lax.broadcasted_iota(jnp.int32, (n, n), 0) == lax.broadcasted_iota(jnp.int32, (n, n), 1)
    return jnp.sum(jnp.where(diagonal, row, 0.0), axis=1, keepdims=True)


def valid_row(valid_ref, a, core, half):
    row = valid_ref[a : a + 1, :].astype(jnp.float32)
    return jnp.where(core == 0, row[:, :half], row[:, half:])


def relative(neighbours_ref, a, k, first):
    return neighbours_ref[a, k] - (first + a) + REACH


def gate(pairing_ref, j, partners):
    if partners == 1:
        column = 1 - lax.axis_index("frame")
    else:
        column = j
    return pairing_ref[0, column].astype(jnp.float32) / 16.0


def entry_pairs(tiles):
    rows = LEVELS * tiles
    for k in range(0, NEIGHBOURS, 2):
        entries = range(k, min(k + 2, NEIGHBOURS))
        yield entries, k * rows, len(entries) * rows


def in_hbm(*arrays):
    return [pltpu.with_memory_space_constraint(z, pltpu.HBM) for z in arrays]


def copies(sources, targets, sems):
    started = [pltpu.make_async_copy(s, t, sems.at[i]) for i, (s, t) in enumerate(zip(sources, targets, strict=True))]
    for copy in started:
        copy.start()
    return started


def side_bases(tiles):
    parity = lax.rem(lax.axis_index("tile"), 2)
    return (1 - parity) * 2 * tiles, parity * 2 * tiles


def shape_of(shape, dtype=jnp.bfloat16):
    return jax.ShapeDtypeStruct(shape, dtype)


def call(kernel, name, outs, in_specs, out_specs, scratch, vmem_mib, aliases=None):
    return pl.pallas_call(
        kernel,
        out_shape=outs,
        in_specs=in_specs,
        out_specs=out_specs,
        scratch_shapes=scratch,
        input_output_aliases=aliases or {},
        compiler_params=pltpu.CompilerParams(vmem_limit_bytes=vmem_mib * 2**20),
        name=name,
    )


def fold_kernel(tiles, half, partners, neighbours_hbm, valid_hbm, pairing_hbm, cot_hbm, features_hbm, *refs):
    folded_ref, x_ref, gates_ref, keep_ref, pool_ref, list_ref = refs[:6]
    neighbours_ref, valid_ref, pairing_ref, cot_ref, stage, sems, *totals = refs[6:]
    core = lax.axis_index("chan")
    first = lax.axis_index("tile") * tiles
    small, (features_copy, list_copy, *waits) = split(
        copies(
            [neighbours_hbm, valid_hbm, pairing_hbm, features_hbm.at[0], neighbours_hbm] + [cot_hbm.at[k] for k in range(NEIGHBOURS)],
            [neighbours_ref, valid_ref, pairing_ref, x_ref, list_ref] + [cot_ref.at[k] for k in range(NEIGHBOURS)],
            sems,
        ),
        3,
    )
    pool_ref[...] = coarse_weights((PAD, PIXELS), 1)
    pool = coarse_weights((PIXELS, PAD), 0)
    for total in totals:
        total[...] = jnp.zeros_like(total)
    for copy in small:
        copy.wait()
    keep = [valid_row(valid_ref, a, core, half) for a in range(tiles)]
    columns = [jnp.broadcast_to(column_of(row), (half, half)) for row in keep]
    for j in range(partners):
        weight = gate(pairing_ref, j, partners)
        gates_ref[j] = jnp.full(gates_ref.shape[1:], weight, jnp.float32)
        for a in range(tiles):
            keep_ref[j, a * half : (a + 1) * half] = columns[a] * weight
    for k, copy in enumerate(waits):
        copy.wait()
        stage[k % STAGES] = cot_ref[k].astype(jnp.float32).reshape(LEVELS * tiles, half)
        for a in range(tiles):
            w = relative(neighbours_ref, a, k, first)
            totals[a][w, :LEVELS] += stage[k % STAGES, pl.ds(a, LEVELS, stride=tiles), :]
    for a in range(tiles):
        for w in range(SPAN):
            coarse = totals[a][w, PIXELS:].astype(jnp.bfloat16)
            spread = jnp.dot(pool, coarse, preferred_element_type=jnp.float32)
            folded_ref[fold_rows(a, w)] = ((totals[a][w, :PIXELS] + spread) * keep[a]).astype(jnp.bfloat16)
    features_copy.wait()
    list_copy.wait()
    _, there = halves(core, half)
    for a in range(tiles):
        folded_ref[query_rows(tiles, half, a)] = x_ref[a, there, :]


def split(items, count):
    return items[:count], items[count:]


def fold_rows(a, w):
    start = (a * SPAN + w) * PIXELS
    return slice(start, start + PIXELS)


def query_rows(tiles, half, a):
    start = tiles * SPAN * PIXELS + a * half
    return slice(start, start + half)


def fold(partners, neighbours, valid, pairing, cotangent, features):
    half = cotangent.shape[-1]
    _, tiles, pixels, channels = features.shape
    return call(
        functools.partial(fold_kernel, tiles, half, partners),
        "fold",
        (
            shape_of((tiles * SPAN * PIXELS + tiles * half, half)),
            shape_of((tiles, pixels, channels)),
            shape_of((partners, 8, channels), jnp.float32),
            shape_of((partners, tiles * half, channels), jnp.float32),
            shape_of((PAD, PIXELS)),
            shape_of(neighbours.shape, jnp.int32),
        ),
        [HBM] * 5,
        (VMEM,) * 6,
        [
            pltpu.SMEM(neighbours.shape, jnp.int32),
            pltpu.VMEM(valid.shape, jnp.int32),
            pltpu.SMEM(pairing.shape, jnp.int32),
            pltpu.VMEM(cotangent.shape, jnp.bfloat16),
            pltpu.VMEM((STAGES, LEVELS * tiles, half), jnp.float32),
            pltpu.SemaphoreType.DMA((5 + NEIGHBOURS,)),
        ]
        + [pltpu.VMEM((SPAN, WIDE, half), jnp.float32)] * tiles,
        10,
    )(*in_hbm(neighbours, valid, pairing, cotangent, features))


def halves(core, half):
    here = pl.ds(pl.multiple_of(core * half, half), half)
    there = pl.ds(pl.multiple_of((1 - core) * half, half), half)
    return here, there


def keys_kernel(tiles, half, x_ref, mine_ref, other_ref, own_ref, even_ref, odd_ref):
    here, there = halves(lax.axis_index("chan"), half)
    queries = [jnp.concatenate([x_ref[a, here, :], x_ref[a, there, :]], axis=0) for a in range(tiles)]

    def of_slot(slot):
        users = [a for a in range(tiles) if 0 <= slot - a < SPAN]
        blocks = [ref[fold_rows(a, slot - a)] for a in users for ref in (mine_ref, other_ref)]
        return jnp.dot(
            jnp.concatenate(blocks, axis=1),
            jnp.concatenate([queries[a] for a in users], axis=0),
            preferred_element_type=jnp.float32,
        )

    parity = lax.rem(lax.axis_index("tile"), 2)
    for a in range(tiles):
        below = of_slot(a).astype(jnp.bfloat16)
        above = of_slot(2 * tiles + a).astype(jnp.bfloat16)
        even_ref[a] = jnp.where(parity == 0, above, below)
        odd_ref[a] = jnp.where(parity == 0, below, above)
        own_ref[a] = of_slot(tiles + a)


def keys(x, mine, other):
    tiles, half = x.shape[0], mine.shape[1]
    return call(
        functools.partial(keys_kernel, tiles, half),
        "keys",
        (shape_of(x.shape, jnp.float32), shape_of(x.shape), shape_of(x.shape)),
        [VMEM] * 3,
        (VMEM,) * 3,
        [],
        4,
    )(x, mine, other)


def returns_kernel(partners, gates_ref, own_ref, even_ref, odd_ref, *out_refs):
    tile, count = lax.axis_index("tile"), lax.axis_size("tile")
    parity = lax.rem(tile, 2)
    has_even = jnp.logical_or(parity == 1, tile + 1 < count)
    has_odd = jnp.logical_or(jnp.logical_and(parity == 0, tile > 0), jnp.logical_and(parity == 1, tile + 1 < count))
    tiles, pixels, _ = own_ref.shape
    for a in range(tiles):
        total = own_ref[a]
        total = total + jnp.where(has_even, even_ref[a].astype(jnp.float32), 0.0)
        total = total + jnp.where(has_odd, odd_ref[a].astype(jnp.float32), 0.0)
        for j in range(partners):
            out_refs[j][a * pixels : (a + 1) * pixels] = (total * gates_ref[j, :1]).astype(jnp.bfloat16)
    for j in range(partners):
        out_refs[j][tiles * pixels :] = jnp.zeros((MARGIN, out_refs[j].shape[1]), jnp.bfloat16)


def returns(partners, gates, own, even, odd):
    tiles, pixels, channels = own.shape
    return call(
        functools.partial(returns_kernel, partners),
        "returns",
        (shape_of((tiles * pixels + MARGIN, channels)),) * partners,
        [VMEM] * 4,
        (VMEM,) * partners,
        [],
        3,
    )(gates, own, even, odd)


def join(mine, other):
    core = lax.axis_index("chan")
    return jnp.concatenate([jnp.where(core == 0, mine, other), jnp.where(core == 0, other, mine)], axis=-1)


def multiply(left, right, contract):
    return lax.dot_general(left, right, ((contract[:1], contract[1:]), ((), ())), preferred_element_type=jnp.float32)


def window_slots(tiles):
    even, odd = side_bases(tiles)
    return tiles, even, odd


def beside_groups(tiles):
    return slice(0, tiles), slice(2 * tiles, 3 * tiles)


def add_scores(tiles, partners, channels, pool, queries_ref, levels, fine_ref, coarse_ref, first):
    for group in beside_groups(tiles):
        fine, coarse = None, None
        for j in range(partners):
            queries = queries_ref[j, channels, :]
            level = levels[j, group]
            width = level.shape[2]
            cells = [jnp.dot(pool, level[a], preferred_element_type=jnp.float32) for a in range(tiles)]
            cells = jnp.concatenate(cells, axis=0).astype(jnp.bfloat16)
            fine_term = multiply(level.reshape(tiles * PIXELS, width), queries, (1, 0))
            coarse_term = multiply(cells, queries, (1, 0))
            fine = fine_term if fine is None else fine + fine_term
            coarse = coarse_term if coarse is None else coarse + coarse_term
        fine = fine.reshape(tiles, PIXELS, fine.shape[1])
        coarse = coarse.reshape(tiles, PAD, coarse.shape[1])
        fine_ref[group] = fine if first else fine_ref[group] + fine
        coarse_ref[group] = coarse if first else coarse_ref[group] + coarse


def sides_kernel(tiles, half, partners, gates_ref, folded_ref, other_ref, pool_ref, queries_ref, near_fine, near_coarse, *refs):
    inputs, (grad_ref, fine_ref, coarse_ref, levels) = refs[: 3 * partners], refs[3 * partners :]
    here, there = halves(lax.axis_index("chan"), half)
    for j in range(partners):
        for part, base in enumerate(window_slots(tiles)):
            levels[j, pl.ds(base, tiles)] = inputs[3 * j + part][...]
    for a in range(tiles):
        grad = None
        for j in range(partners):
            term = None
            for w in range(SPAN):
                both = jnp.concatenate([folded_ref[fold_rows(a, w)], other_ref[fold_rows(a, w)]], axis=1)
                part = multiply(both, levels[j, a + w], (0, 0))
                term = part if term is None else term + part
            term = term * gates_ref[j, :1]
            grad = term if grad is None else grad + term
        grad_ref[a, here, :] = grad[:half]
        grad_ref[a, there, :] = grad[half:]
    mine, _ = halves(lax.axis_index("chan"), grad_ref.shape[2])
    add_scores(tiles, partners, mine, pool_ref[...], queries_ref, levels, fine_ref, coarse_ref, True)


def sides(partners, gates, folded, other, pool, queries, fine, coarse, windows):
    tiles, pixels, channels = windows[0].shape
    return call(
        functools.partial(sides_kernel, tiles, pixels // 2, partners),
        "sides",
        (shape_of(windows[0].shape, jnp.float32), shape_of(fine.shape, jnp.float32), shape_of(coarse.shape, jnp.float32)),
        [VMEM] * (7 + len(windows)),
        (VMEM,) * 3,
        [pltpu.VMEM((partners, 3 * tiles, pixels, channels), jnp.bfloat16)],
        6,
        {5: 1, 6: 2},
    )(gates, folded, other, pool, queries, fine, coarse, *windows)


def near_kernel(tiles, half, partners, keep_ref, pool_ref, x_ref, other_ref, *refs):
    same, (queries_ref, fine_ref, coarse_ref) = refs[: 2 * partners], refs[2 * partners :]
    here, _ = halves(lax.axis_index("chan"), half)
    mine = jnp.concatenate([x_ref[a, here, :] for a in range(tiles)], axis=0).astype(jnp.float32)
    other = jnp.concatenate([other_ref[query_rows(tiles, half, a)] for a in range(tiles)], axis=0).astype(jnp.float32)
    pool = pool_ref[...]
    for j in range(partners):
        queries_ref[j] = join(mine * keep_ref[j], other * keep_ref[j]).T.astype(jnp.bfloat16)
    for s in range(tiles):
        fine, coarse = None, None
        for j in range(partners):
            level = join(same[2 * j][s], same[2 * j + 1][s])
            cells = jnp.dot(pool, level, preferred_element_type=jnp.float32).astype(jnp.bfloat16)
            fine_term = multiply(level, queries_ref[j], (1, 0))
            coarse_term = multiply(cells, queries_ref[j], (1, 0))
            fine = fine_term if fine is None else fine + fine_term
            coarse = coarse_term if coarse is None else coarse + coarse_term
        fine_ref[tiles + s] = fine
        coarse_ref[tiles + s] = coarse


def near(partners, keep, pool, x, other, same):
    tiles, pixels, channels = x.shape
    return call(
        functools.partial(near_kernel, tiles, pixels // 2, partners),
        "near",
        (
            shape_of((partners, 2 * channels, tiles * pixels // 2)),
            shape_of((3 * tiles, pixels, tiles * pixels // 2), jnp.float32),
            shape_of((3 * tiles, PAD, tiles * pixels // 2), jnp.float32),
        ),
        [VMEM] * (4 + len(same)),
        (VMEM,) * 3,
        [],
        6,
    )(keep, pool, x, other, *same)


def volume_kernel(tiles, half, partners, list_ref, queries_ref, pool_ref, part_ref, near_fine, near_coarse, *refs):
    inputs, returned, rest = refs[: 2 * partners], refs[2 * partners : 3 * partners], refs[3 * partners :]
    volume_hbm, grad_hbm, fine_table, coarse_table, levels, stage, volume_ref, grad_ref, sems = rest
    first = lax.axis_index("tile") * tiles
    listed = list_ref[...]
    pixels, channels = grad_ref.shape[1:]
    for a in range(tiles):
        summed = part_ref[a]
        for j in range(partners):
            summed = summed + returned[j][a * pixels : (a + 1) * pixels].astype(jnp.float32)
        grad_ref[a] = summed
    waits = [pltpu.make_async_copy(grad_ref, grad_hbm.at[0], sems.at[0])]
    waits[0].start()
    for j in range(partners):
        for part, base in enumerate(side_bases(tiles)):
            levels[j, pl.ds(base, tiles)] = inputs[2 * j + part][...]
    _, other = halves(lax.axis_index("chan"), channels)
    add_scores(tiles, partners, other, pool_ref[...], queries_ref, levels, fine_table, coarse_table, False)
    for i_part, (entries, start, size) in enumerate(entry_pairs(tiles)):
        for i, k in enumerate(entries):
            for a in range(tiles):
                slot = relative(listed, a, k, first) + a
                lanes = slice(a * half, (a + 1) * half)
                base = i * LEVELS * tiles + a
                stage[pl.ds(base, PIXELS, stride=tiles), :] = fine_table[slot, :, lanes]
                stage[pl.ds(base + PIXELS * tiles, COARSE, stride=tiles), :] = coarse_table[slot, :COARSE, lanes]
        rows = pl.ds(start, size)
        volume_ref[rows, :] = stage[:size].astype(jnp.bfloat16)
        copy = pltpu.make_async_copy(volume_ref.at[rows], volume_hbm.at[rows], sems.at[1 + i_part])
        copy.start()
        waits.append(copy)
    for copy in waits:
        copy.wait()


def volumes(partners, neighbours, queries, pool, grad, fine, coarse, beside, returned):
    tiles, pixels, channels = grad.shape
    half = pixels // 2
    rows = NEIGHBOURS * LEVELS * tiles
    volume, feature_grad, _, _ = call(
        functools.partial(volume_kernel, tiles, half, partners),
        "volume",
        (
            shape_of((rows, half)),
            shape_of((1,) + grad.shape, jnp.float32),
            shape_of(fine.shape, jnp.float32),
            shape_of(coarse.shape, jnp.float32),
        ),
        [VMEM] * (6 + len(beside) + len(returned)),
        (HBM, HBM, VMEM, VMEM),
        [
            pltpu.VMEM((partners, 3 * tiles, pixels, channels), jnp.bfloat16),
            pltpu.VMEM((2 * LEVELS * tiles, half), jnp.float32),
            pltpu.VMEM((rows, half), jnp.bfloat16),
            pltpu.VMEM(grad.shape, jnp.float32),
            pltpu.SemaphoreType.DMA((1 + (NEIGHBOURS + 1) // 2,)),
        ],
        8,
        {4: 2, 5: 3},
    )(neighbours, queries, pool, grad, fine, coarse, *beside, *returned)
    return volume, feature_grad


def after(value, earlier):
    return lax.optimization_barrier((value, earlier))[0]


def local(features, neighbours, pairing, valid_tiles, cotangent):
    count = lax.axis_size("tile")
    cores = lax.axis_size("chan")
    links = frame_links(lax.axis_size("frame"))
    partners = len(links)
    tiles, half = cotangent.shape[1:3]
    swap = [(c, (c + 1) % cores) for c in range(cores)]
    evens, odds = even_pairs(count), odd_pairs(count, cores)

    def over_even(z):
        return lax.ppermute(z, "tile", evens)

    def over_odd(z):
        return lax.ppermute(z, ("tile", "chan"), odds)

    def over_cores(z):
        return lax.ppermute(z, "chan", swap)

    upstream = jnp.transpose(cotangent[0], (2, 0, 1)).reshape(NEIGHBOURS, LEVELS * tiles // 8, 8, half)
    folded, x, gates, keep, pool, listed = fold(partners, neighbours, valid_tiles, pairing, upstream, features)
    other = over_cores(folded)
    arrived = [lax.ppermute(x, "frame", ahead) for ahead, _ in links]
    own, to_even, to_odd = keys(x, folded, other)
    arrived = [after(y, own) for y in arrived]
    beside = [(over_even(y), over_odd(y)) for y in arrived]
    from_odd = over_odd(to_odd)
    from_even = after(over_even(to_even), from_odd)
    sent = returns(partners, gates, own, from_even, from_odd)
    returned = [lax.ppermute(z, "frame", back) for z, (_, back) in zip(sent, links, strict=True)]
    same = []
    for y in arrived:
        same += [after(y, sent[0]), after(over_cores(y), sent[0])]
    queries, fine, coarse = near(partners, keep, pool, x, other, same)
    mine, exchanged = [], []
    for y, (even, odd) in zip(arrived, beside, strict=True):
        even, odd = after(even, fine), after(odd, fine)
        mine += [y, even, odd]
        exchanged += [over_cores(even), over_cores(odd)]
    grad, fine, coarse = sides(partners, gates, folded, other, pool, queries, fine, coarse, mine)
    exchanged = [after(z, grad) for z in exchanged]
    volume, feature_grad = volumes(partners, listed, queries, pool, grad, fine, coarse, exchanged, returned)
    volume = jnp.transpose(volume.reshape(NEIGHBOURS * LEVELS, tiles, half), (1, 2, 0))
    return volume[None], feature_grad


def solution(mesh):
    return jax.shard_map(
        local,
        mesh=mesh,
        in_specs=(
            P(("clip", "frame"), "tile", None, "chan"),
            P(("clip", "tile"), None),
            P(("clip", "frame"), None),
            P(("clip", "tile"), None),
            P(("clip", "frame"), "tile", "chan", None),
        ),
        out_specs=(
            P(("clip", "frame"), "tile", "chan", None),
            P(("clip", "frame"), "tile", None, "chan"),
        ),
        check_vma=False,
    )
```

```python
import functools

import jax
import jax.numpy as jnp
from jax import lax
from jax.experimental import pallas as pl
from jax.experimental.pallas import tpu as pltpu
from jax.sharding import PartitionSpec as P

CHANNELS = 256
SIDE = 16
PIXELS = 256
LEVELS = 340
NEIGHBOURS = 9
REACH = 2
SPAN = 2 * REACH + 1
COARSE = LEVELS - PIXELS
MARGIN = 16
STAGES = 9
PAD = 128
WIDE = PIXELS + PAD

VMEM = pl.BlockSpec(memory_space=pltpu.VMEM)
HBM = pl.BlockSpec(memory_space=pltpu.HBM)


def even_pairs(count):
    pairs = []
    for i in range(0, count - 1, 2):
        pairs += [(i, i + 1), (i + 1, i)]
    if count % 2:
        pairs.append((count - 1, count - 1))
    return pairs


def odd_pairs(count, cores):
    pairs, paired = [], set()
    for i in range(1, count - 1, 2):
        paired |= {i, i + 1}
        for c in range(cores):
            pairs += [(i * cores + c, (i + 1) * cores + c), ((i + 1) * cores + c, i * cores + c)]
    for i in range(count):
        if i not in paired:
            pairs += [(i * cores + c, i * cores + (c + 1) % cores) for c in range(cores)]
    return pairs


def frame_links(count):
    if count == 2:
        swap = [(0, 1), (1, 0)]
        return [(swap, swap)]
    onward = [(i, i + 1) for i in range(count - 1)]
    back = [(i + 1, i) for i in range(count - 1)]
    return [(onward, back), (back, onward)]


def coarse_weights(shape, pixel_axis):
    pixel = lax.broadcasted_iota(jnp.int32, shape, pixel_axis)
    cell = lax.broadcasted_iota(jnp.int32, shape, 1 - pixel_axis)
    row, column = lax.shift_right_logical(pixel, 4), jnp.bitwise_and(pixel, SIDE - 1)
    table = jnp.zeros(shape, jnp.float32)
    base = 0
    for level, across in ((1, 8), (2, 4), (3, 2)):
        target = base + lax.shift_right_logical(row, level) * across + lax.shift_right_logical(column, level)
        table = jnp.where(cell == target, 0.25**level, table)
        base += across * across
    return table.astype(jnp.bfloat16)


def column_of(row):
    n = row.shape[1]
    diagonal = lax.broadcasted_iota(jnp.int32, (n, n), 0) == lax.broadcasted_iota(jnp.int32, (n, n), 1)
    return jnp.sum(jnp.where(diagonal, row, 0.0), axis=1, keepdims=True)


def valid_row(valid_ref, a, core, half):
    row = valid_ref[a : a + 1, :].astype(jnp.float32)
    return jnp.where(core == 0, row[:, :half], row[:, half:])


def relative(neighbours_ref, a, k, first):
    return neighbours_ref[a, k] - (first + a) + REACH


def gate(pairing_ref, j, partners):
    if partners == 1:
        column = 1 - lax.axis_index("frame")
    else:
        column = j
    return pairing_ref[0, column].astype(jnp.float32) / 16.0


def entry_pairs(tiles):
    rows = LEVELS * tiles
    for k in range(0, NEIGHBOURS, 2):
        entries = range(k, min(k + 2, NEIGHBOURS))
        yield entries, k * rows, len(entries) * rows


def in_hbm(*arrays):
    return [pltpu.with_memory_space_constraint(z, pltpu.HBM) for z in arrays]


def copies(sources, targets, sems):
    started = [pltpu.make_async_copy(s, t, sems.at[i]) for i, (s, t) in enumerate(zip(sources, targets, strict=True))]
    for copy in started:
        copy.start()
    return started


def side_bases(tiles):
    parity = lax.rem(lax.axis_index("tile"), 2)
    return (1 - parity) * 2 * tiles, parity * 2 * tiles


def shape_of(shape, dtype=jnp.bfloat16):
    return jax.ShapeDtypeStruct(shape, dtype)


def call(kernel, name, outs, in_specs, out_specs, scratch, vmem_mib, aliases=None):
    return pl.pallas_call(
        kernel,
        out_shape=outs,
        in_specs=in_specs,
        out_specs=out_specs,
        scratch_shapes=scratch,
        input_output_aliases=aliases or {},
        compiler_params=pltpu.CompilerParams(vmem_limit_bytes=vmem_mib * 2**20),
        name=name,
    )


def fold_kernel(tiles, half, partners, neighbours_hbm, valid_hbm, pairing_hbm, cot_hbm, features_hbm, *refs):
    folded_ref, x_ref, gates_ref, keep_ref, pool_ref, list_ref = refs[:6]
    neighbours_ref, valid_ref, pairing_ref, cot_ref, stage, sems, *totals = refs[6:]
    core = lax.axis_index("chan")
    first = lax.axis_index("tile") * tiles
    small, (features_copy, list_copy, *waits) = split(
        copies(
            [neighbours_hbm, valid_hbm, pairing_hbm, features_hbm.at[0], neighbours_hbm] + [cot_hbm.at[k] for k in range(NEIGHBOURS)],
            [neighbours_ref, valid_ref, pairing_ref, x_ref, list_ref] + [cot_ref.at[k] for k in range(NEIGHBOURS)],
            sems,
        ),
        3,
    )
    pool_ref[...] = coarse_weights((PAD, PIXELS), 1)
    pool = coarse_weights((PIXELS, PAD), 0)
    for total in totals:
        total[...] = jnp.zeros_like(total)
    for copy in small:
        copy.wait()
    keep = [valid_row(valid_ref, a, core, half) for a in range(tiles)]
    columns = [jnp.broadcast_to(column_of(row), (half, half)) for row in keep]
    for j in range(partners):
        weight = gate(pairing_ref, j, partners)
        gates_ref[j] = jnp.full(gates_ref.shape[1:], weight, jnp.float32)
        for a in range(tiles):
            keep_ref[j, a * half : (a + 1) * half] = columns[a] * weight
    for k, copy in enumerate(waits):
        copy.wait()
        stage[k % STAGES] = cot_ref[k].astype(jnp.float32).reshape(LEVELS * tiles, half)
        for a in range(tiles):
            w = relative(neighbours_ref, a, k, first)
            totals[a][w, :LEVELS] += stage[k % STAGES, pl.ds(a, LEVELS, stride=tiles), :]
    for a in range(tiles):
        for w in range(SPAN):
            coarse = totals[a][w, PIXELS:].astype(jnp.bfloat16)
            spread = jnp.dot(pool, coarse, preferred_element_type=jnp.float32)
            folded_ref[fold_rows(a, w)] = ((totals[a][w, :PIXELS] + spread) * keep[a]).astype(jnp.bfloat16)
    features_copy.wait()
    list_copy.wait()
    _, there = halves(core, half)
    for a in range(tiles):
        folded_ref[query_rows(tiles, half, a)] = x_ref[a, there, :]


def split(items, count):
    return items[:count], items[count:]


def fold_rows(a, w):
    start = (a * SPAN + w) * PIXELS
    return slice(start, start + PIXELS)


def query_rows(tiles, half, a):
    start = tiles * SPAN * PIXELS + a * half
    return slice(start, start + half)


def fold(partners, neighbours, valid, pairing, cotangent, features):
    half = cotangent.shape[-1]
    _, tiles, pixels, channels = features.shape
    return call(
        functools.partial(fold_kernel, tiles, half, partners),
        "fold",
        (
            shape_of((tiles * SPAN * PIXELS + tiles * half, half)),
            shape_of((tiles, pixels, channels)),
            shape_of((partners, 8, channels), jnp.float32),
            shape_of((partners, tiles * half, channels), jnp.float32),
            shape_of((PAD, PIXELS)),
            shape_of(neighbours.shape, jnp.int32),
        ),
        [HBM] * 5,
        (VMEM,) * 6,
        [
            pltpu.SMEM(neighbours.shape, jnp.int32),
            pltpu.VMEM(valid.shape, jnp.int32),
            pltpu.SMEM(pairing.shape, jnp.int32),
            pltpu.VMEM(cotangent.shape, jnp.bfloat16),
            pltpu.VMEM((STAGES, LEVELS * tiles, half), jnp.float32),
            pltpu.SemaphoreType.DMA((5 + NEIGHBOURS,)),
        ]
        + [pltpu.VMEM((SPAN, WIDE, half), jnp.float32)] * tiles,
        10,
    )(*in_hbm(neighbours, valid, pairing, cotangent, features))


def halves(core, half):
    here = pl.ds(pl.multiple_of(core * half, half), half)
    there = pl.ds(pl.multiple_of((1 - core) * half, half), half)
    return here, there


def window_grad(tiles, slot, queries, folded_ref):
    users = [a for a in range(tiles) if 0 <= slot - a < SPAN]
    blocks = [folded_ref[fold_rows(a, slot - a)] for a in users]
    return jnp.dot(
        jnp.concatenate(blocks, axis=1),
        jnp.concatenate([queries[a] for a in users], axis=0),
        preferred_element_type=jnp.float32,
    )


def early_kernel(tiles, half, x_ref, mine_ref, part_ref):
    here, _ = halves(lax.axis_index("chan"), half)
    queries = [x_ref[a, here, :] for a in range(tiles)]
    for slot in range(3 * tiles):
        part_ref[slot] = window_grad(tiles, slot, queries, mine_ref)


def early(x, mine):
    tiles, pixels, channels = x.shape
    return call(
        functools.partial(early_kernel, tiles, mine.shape[1]),
        "early",
        shape_of((3 * tiles, pixels, channels), jnp.float32),
        [VMEM] * 2,
        VMEM,
        [],
        4,
    )(x, mine)


def keys_kernel(tiles, half, x_ref, part_ref, other_ref, own_ref, even_ref, odd_ref):
    _, there = halves(lax.axis_index("chan"), half)
    queries = [x_ref[a, there, :] for a in range(tiles)]

    def of_slot(slot):
        return part_ref[slot] + window_grad(tiles, slot, queries, other_ref)

    parity = lax.rem(lax.axis_index("tile"), 2)
    for a in range(tiles):
        below = of_slot(a).astype(jnp.bfloat16)
        above = of_slot(2 * tiles + a).astype(jnp.bfloat16)
        even_ref[a] = jnp.where(parity == 0, above, below)
        odd_ref[a] = jnp.where(parity == 0, below, above)
        own_ref[a] = of_slot(tiles + a)


def keys(x, part, other):
    tiles, half = x.shape[0], other.shape[1]
    return call(
        functools.partial(keys_kernel, tiles, half),
        "keys",
        (shape_of(x.shape, jnp.float32), shape_of(x.shape), shape_of(x.shape)),
        [VMEM] * 3,
        (VMEM,) * 3,
        [],
        4,
    )(x, part, other)


def returns_kernel(partners, gates_ref, own_ref, even_ref, odd_ref, *out_refs):
    tile, count = lax.axis_index("tile"), lax.axis_size("tile")
    parity = lax.rem(tile, 2)
    has_even = jnp.logical_or(parity == 1, tile + 1 < count)
    has_odd = jnp.logical_or(jnp.logical_and(parity == 0, tile > 0), jnp.logical_and(parity == 1, tile + 1 < count))
    tiles, pixels, _ = own_ref.shape
    for a in range(tiles):
        total = own_ref[a]
        total = total + jnp.where(has_even, even_ref[a].astype(jnp.float32), 0.0)
        total = total + jnp.where(has_odd, odd_ref[a].astype(jnp.float32), 0.0)
        for j in range(partners):
            out_refs[j][a * pixels : (a + 1) * pixels] = (total * gates_ref[j, :1]).astype(jnp.bfloat16)
    for j in range(partners):
        out_refs[j][tiles * pixels :] = jnp.zeros((MARGIN, out_refs[j].shape[1]), jnp.bfloat16)


def returns(partners, gates, own, even, odd):
    tiles, pixels, channels = own.shape
    return call(
        functools.partial(returns_kernel, partners),
        "returns",
        (shape_of((tiles * pixels + MARGIN, channels)),) * partners,
        [VMEM] * 4,
        (VMEM,) * partners,
        [],
        3,
    )(gates, own, even, odd)


def join(mine, other):
    core = lax.axis_index("chan")
    return jnp.concatenate([jnp.where(core == 0, mine, other), jnp.where(core == 0, other, mine)], axis=-1)


def multiply(left, right, contract):
    return lax.dot_general(left, right, ((contract[:1], contract[1:]), ((), ())), preferred_element_type=jnp.float32)


def query_grads(gates_ref, folded_ref, other_ref, tiles, partners, level_of, slots):
    grads = []
    for a in range(tiles):
        grad = None
        for j in range(partners):
            term = None
            for slot in slots:
                if 0 <= slot - a < SPAN:
                    rows = fold_rows(a, slot - a)
                    both = jnp.concatenate([folded_ref[rows], other_ref[rows]], axis=1)
                    part = multiply(both, level_of(j, slot), (0, 0))
                    term = part if term is None else term + part
            term = term * gates_ref[j, :1]
            grad = term if grad is None else grad + term
        grads.append(grad)
    return grads


def ready_kernel(tiles, half, partners, gates_ref, keep_ref, x_ref, folded_ref, other_ref, *refs):
    same, (queries_ref, grad_ref) = refs[:partners], refs[partners:]
    here, _ = halves(lax.axis_index("chan"), half)
    mine = jnp.concatenate([x_ref[a, here, :] for a in range(tiles)], axis=0).astype(jnp.float32)
    other = jnp.concatenate([other_ref[query_rows(tiles, half, a)] for a in range(tiles)], axis=0).astype(jnp.float32)
    for j in range(partners):
        queries_ref[j] = join(mine * keep_ref[j], other * keep_ref[j]).T.astype(jnp.bfloat16)
    slots = range(tiles, 2 * tiles)
    grads = query_grads(
        gates_ref, folded_ref, other_ref, tiles, partners, lambda j, slot: same[j][slot - tiles], slots
    )
    for a in range(tiles):
        grad_ref[a] = grads[a]


def ready(partners, gates, keep, x, folded, other, same):
    tiles, pixels, channels = x.shape
    return call(
        functools.partial(ready_kernel, tiles, pixels // 2, partners),
        "ready",
        (shape_of((partners, 2 * channels, tiles * pixels // 2)), shape_of(x.shape, jnp.float32)),
        [VMEM] * (5 + len(same)),
        (VMEM,) * 2,
        [],
        6,
    )(gates, keep, x, folded, other, *same)


def sides_kernel(tiles, half, partners, gates_ref, folded_ref, other_ref, part_ref, *refs):
    inputs, (grad_ref, levels) = refs[: 2 * partners], refs[2 * partners :]
    here, there = halves(lax.axis_index("chan"), half)
    for j in range(partners):
        for part, base in enumerate(side_bases(tiles)):
            levels[j, pl.ds(base, tiles)] = inputs[2 * j + part][...]
    slots = [slot for slot in range(3 * tiles) if not tiles <= slot < 2 * tiles]
    grads = query_grads(
        gates_ref, folded_ref, other_ref, tiles, partners, lambda j, slot: levels[j, slot], slots
    )
    for a in range(tiles):
        grad = part_ref[a] + grads[a]
        grad_ref[a, here, :] = grad[:half]
        grad_ref[a, there, :] = grad[half:]


def sides(partners, gates, folded, other, part, windows):
    tiles, pixels, channels = windows[0].shape
    return call(
        functools.partial(sides_kernel, tiles, pixels // 2, partners),
        "sides",
        shape_of(windows[0].shape, jnp.float32),
        [VMEM] * (4 + len(windows)),
        VMEM,
        [pltpu.VMEM((partners, 3 * tiles, pixels, channels), jnp.bfloat16)],
        6,
    )(gates, folded, other, part, *windows)


def near_kernel(tiles, partners, queries_ref, pool_ref, *refs):
    same, (fine_ref, coarse_ref) = refs[: 2 * partners], refs[2 * partners :]
    pool = pool_ref[...]
    for s in range(tiles):
        fine, coarse = None, None
        for j in range(partners):
            level = join(same[2 * j][s], same[2 * j + 1][s])
            cells = jnp.dot(pool, level, preferred_element_type=jnp.float32).astype(jnp.bfloat16)
            fine_term = multiply(level, queries_ref[j], (1, 0))
            coarse_term = multiply(cells, queries_ref[j], (1, 0))
            fine = fine_term if fine is None else fine + fine_term
            coarse = coarse_term if coarse is None else coarse + coarse_term
        fine_ref[tiles + s] = fine
        coarse_ref[tiles + s] = coarse


def near(partners, queries, pool, same):
    tiles, pixels, _ = same[0].shape
    return call(
        functools.partial(near_kernel, tiles, partners),
        "near",
        (
            shape_of((3 * tiles, pixels, tiles * pixels // 2), jnp.float32),
            shape_of((3 * tiles, PAD, tiles * pixels // 2), jnp.float32),
        ),
        [VMEM] * (2 + len(same)),
        (VMEM,) * 2,
        [],
        6,
    )(queries, pool, *same)


def tables_kernel(tiles, partners, queries_ref, pool_ref, near_fine, near_coarse, *refs):
    inputs, (fine_table, coarse_table, levels, cells) = refs[: 4 * partners], refs[4 * partners :]
    pool = pool_ref[...]
    for j in range(partners):
        for part in range(2):
            for a in range(tiles):
                level = join(inputs[4 * j + part][a], inputs[4 * j + 2 + part][a])
                at = part * tiles + a
                levels[j, at * PIXELS : (at + 1) * PIXELS] = level
                cells[j, at * PAD : (at + 1) * PAD] = jnp.dot(
                    pool, level, preferred_element_type=jnp.float32
                ).astype(jnp.bfloat16)
    for keys_at, table in ((levels, fine_table), (cells, coarse_table)):
        scores = multiply(keys_at[0], queries_ref[0], (1, 0))
        for j in range(1, partners):
            scores = scores + multiply(keys_at[j], queries_ref[j], (1, 0))
        scores = scores.reshape(2, tiles, table.shape[1], table.shape[2])
        for part, base in enumerate(side_bases(tiles)):
            table[pl.ds(base, tiles)] = scores[part]


def tables(partners, queries, pool, fine, coarse, beside):
    tiles, pixels, channels = beside[0].shape
    return call(
        functools.partial(tables_kernel, tiles, partners),
        "tables",
        (shape_of(fine.shape, jnp.float32), shape_of(coarse.shape, jnp.float32)),
        [VMEM] * (4 + len(beside)),
        (VMEM,) * 2,
        [
            pltpu.VMEM((partners, 2 * tiles * pixels, 2 * channels), jnp.bfloat16),
            pltpu.VMEM((partners, 2 * tiles * PAD, 2 * channels), jnp.bfloat16),
        ],
        6,
        {2: 0, 3: 1},
    )(queries, pool, fine, coarse, *beside)


def volume_kernel(tiles, half, partners, list_ref, part_ref, fine_table, coarse_table, *refs):
    returned, (volume_hbm, grad_hbm, stage, volume_ref, grad_ref, sems) = refs[:partners], refs[partners:]
    first = lax.axis_index("tile") * tiles
    listed = list_ref[...]
    pixels, channels = grad_ref.shape[1:]
    for a in range(tiles):
        summed = part_ref[a]
        for j in range(partners):
            summed = summed + returned[j][a * pixels : (a + 1) * pixels].astype(jnp.float32)
        grad_ref[a] = summed
    waits = [pltpu.make_async_copy(grad_ref, grad_hbm.at[0], sems.at[0])]
    waits[0].start()
    for i_part, (entries, start, size) in enumerate(entry_pairs(tiles)):
        for i, k in enumerate(entries):
            for a in range(tiles):
                slot = relative(listed, a, k, first) + a
                lanes = slice(a * half, (a + 1) * half)
                base = i * LEVELS * tiles + a
                stage[pl.ds(base, PIXELS, stride=tiles), :] = fine_table[slot, :, lanes]
                stage[pl.ds(base + PIXELS * tiles, COARSE, stride=tiles), :] = coarse_table[slot, :COARSE, lanes]
        rows = pl.ds(start, size)
        volume_ref[rows, :] = stage[:size].astype(jnp.bfloat16)
        copy = pltpu.make_async_copy(volume_ref.at[rows], volume_hbm.at[rows], sems.at[1 + i_part])
        copy.start()
        waits.append(copy)
    for copy in waits:
        copy.wait()


def volumes(partners, neighbours, grad, fine, coarse, returned):
    tiles, pixels, _ = grad.shape
    half = pixels // 2
    rows = NEIGHBOURS * LEVELS * tiles
    return call(
        functools.partial(volume_kernel, tiles, half, partners),
        "volume",
        (shape_of((rows, half)), shape_of((1,) + grad.shape, jnp.float32)),
        [VMEM] * (4 + len(returned)),
        (HBM, HBM),
        [
            pltpu.VMEM((2 * LEVELS * tiles, half), jnp.float32),
            pltpu.VMEM((rows, half), jnp.bfloat16),
            pltpu.VMEM(grad.shape, jnp.float32),
            pltpu.SemaphoreType.DMA((1 + (NEIGHBOURS + 1) // 2,)),
        ],
        8,
    )(neighbours, grad, fine, coarse, *returned)


def after(value, earlier):
    return lax.optimization_barrier((value, earlier))[0]


def local(features, neighbours, pairing, valid_tiles, cotangent):
    count = lax.axis_size("tile")
    cores = lax.axis_size("chan")
    links = frame_links(lax.axis_size("frame"))
    partners = len(links)
    tiles, half = cotangent.shape[1:3]
    swap = [(c, (c + 1) % cores) for c in range(cores)]
    evens, odds = even_pairs(count), odd_pairs(count, cores)

    def over_even(z):
        return lax.ppermute(z, "tile", evens)

    def over_odd(z):
        return lax.ppermute(z, ("tile", "chan"), odds)

    def over_cores(z):
        return lax.ppermute(z, "chan", swap)

    upstream = jnp.transpose(cotangent[0], (2, 0, 1)).reshape(NEIGHBOURS, LEVELS * tiles // 8, 8, half)
    folded, x, gates, keep, pool, listed = fold(partners, neighbours, valid_tiles, pairing, upstream, features)
    other = over_cores(folded)
    arrived = [lax.ppermute(x, "frame", ahead) for ahead, _ in links]
    own, to_even, to_odd = keys(x, early(x, folded), other)
    arrived = [after(y, own) for y in arrived]
    beside = [(over_even(y), over_odd(y)) for y in arrived]
    from_odd = over_odd(to_odd)
    from_even = after(over_even(to_even), from_odd)
    sent = returns(partners, gates, own, from_even, from_odd)
    returned = [lax.ppermute(z, "frame", back) for z, (_, back) in zip(sent, links, strict=True)]
    queries, part = ready(partners, gates, keep, x, folded, other, [after(y, sent[0]) for y in arrived])
    same, mine, exchanged = [], [], []
    for y, (even, odd) in zip(arrived, beside, strict=True):
        even, odd = after(even, part), after(odd, part)
        same += [after(y, odd), after(over_cores(y), odd)]
        mine += [even, odd]
        exchanged += [even, odd, over_cores(even), over_cores(odd)]
    grad = sides(partners, gates, folded, other, part, mine)
    fine, coarse = near(partners, queries, pool, [after(z, grad) for z in same])
    exchanged = [after(after(z, grad), fine) for z in exchanged]
    fine, coarse = tables(partners, queries, pool, fine, coarse, exchanged)
    returned = [after(z, fine) for z in returned]
    volume, feature_grad = volumes(partners, listed, grad, fine, coarse, returned)
    volume = jnp.transpose(volume.reshape(NEIGHBOURS * LEVELS, tiles, half), (1, 2, 0))
    return volume[None], feature_grad


def solution(mesh):
    return jax.shard_map(
        local,
        mesh=mesh,
        in_specs=(
            P(("clip", "frame"), "tile", None, "chan"),
            P(("clip", "tile"), None),
            P(("clip", "frame"), None),
            P(("clip", "tile"), None),
            P(("clip", "frame"), "tile", "chan", None),
        ),
        out_specs=(
            P(("clip", "frame"), "tile", "chan", None),
            P(("clip", "frame"), "tile", None, "chan"),
        ),
        check_vma=False,
    )
```

```python
import functools

import jax
import jax.numpy as jnp
from jax import lax
from jax.experimental import pallas as pl
from jax.experimental.pallas import tpu as pltpu
from jax.sharding import PartitionSpec as P

CHANNELS = 256
SIDE = 16
PIXELS = 256
LEVELS = 340
NEIGHBOURS = 9
REACH = 2
SPAN = 2 * REACH + 1
COARSE = LEVELS - PIXELS
MARGIN = 16
STAGES = 9
PAD = 128
WIDE = PIXELS + PAD

VMEM = pl.BlockSpec(memory_space=pltpu.VMEM)
HBM = pl.BlockSpec(memory_space=pltpu.HBM)


def even_pairs(count):
    pairs = []
    for i in range(0, count - 1, 2):
        pairs += [(i, i + 1), (i + 1, i)]
    if count % 2:
        pairs.append((count - 1, count - 1))
    return pairs


def odd_pairs(count, cores):
    pairs, paired = [], set()
    for i in range(1, count - 1, 2):
        paired |= {i, i + 1}
        for c in range(cores):
            pairs += [(i * cores + c, (i + 1) * cores + c), ((i + 1) * cores + c, i * cores + c)]
    for i in range(count):
        if i not in paired:
            pairs += [(i * cores + c, i * cores + (c + 1) % cores) for c in range(cores)]
    return pairs


def frame_links(count):
    if count == 2:
        swap = [(0, 1), (1, 0)]
        return [(swap, swap)]
    onward = [(i, i + 1) for i in range(count - 1)]
    back = [(i + 1, i) for i in range(count - 1)]
    return [(onward, back), (back, onward)]


def coarse_weights(shape, pixel_axis):
    pixel = lax.broadcasted_iota(jnp.int32, shape, pixel_axis)
    cell = lax.broadcasted_iota(jnp.int32, shape, 1 - pixel_axis)
    row, column = lax.shift_right_logical(pixel, 4), jnp.bitwise_and(pixel, SIDE - 1)
    table = jnp.zeros(shape, jnp.float32)
    base = 0
    for level, across in ((1, 8), (2, 4), (3, 2)):
        target = base + lax.shift_right_logical(row, level) * across + lax.shift_right_logical(column, level)
        table = jnp.where(cell == target, 0.25**level, table)
        base += across * across
    return table.astype(jnp.bfloat16)


def column_of(row):
    n = row.shape[1]
    diagonal = lax.broadcasted_iota(jnp.int32, (n, n), 0) == lax.broadcasted_iota(jnp.int32, (n, n), 1)
    return jnp.sum(jnp.where(diagonal, row, 0.0), axis=1, keepdims=True)


def valid_row(valid_ref, a, core, half):
    row = valid_ref[a : a + 1, :].astype(jnp.float32)
    return jnp.where(core == 0, row[:, :half], row[:, half:])


def relative(neighbours_ref, a, k, first):
    return neighbours_ref[a, k] - (first + a) + REACH


def gate(pairing_ref, j, partners):
    if partners == 1:
        column = 1 - lax.axis_index("frame")
    else:
        column = j
    return pairing_ref[0, column].astype(jnp.float32) / 16.0


def entry_pairs(tiles):
    rows = LEVELS * tiles
    for k in range(0, NEIGHBOURS, 2):
        entries = range(k, min(k + 2, NEIGHBOURS))
        yield entries, k * rows, len(entries) * rows


def in_hbm(*arrays):
    return [pltpu.with_memory_space_constraint(z, pltpu.HBM) for z in arrays]


def copies(sources, targets, sems):
    started = [pltpu.make_async_copy(s, t, sems.at[i]) for i, (s, t) in enumerate(zip(sources, targets, strict=True))]
    for copy in started:
        copy.start()
    return started


def side_bases(tiles):
    parity = lax.rem(lax.axis_index("tile"), 2)
    return (1 - parity) * 2 * tiles, parity * 2 * tiles


def shape_of(shape, dtype=jnp.bfloat16):
    return jax.ShapeDtypeStruct(shape, dtype)


def call(kernel, name, outs, in_specs, out_specs, scratch, vmem_mib):
    return pl.pallas_call(
        kernel,
        out_shape=outs,
        in_specs=in_specs,
        out_specs=out_specs,
        scratch_shapes=scratch,
        compiler_params=pltpu.CompilerParams(vmem_limit_bytes=vmem_mib * 2**20),
        name=name,
    )


def fold_kernel(tiles, half, partners, neighbours_hbm, valid_hbm, pairing_hbm, cot_hbm, features_hbm, *refs):
    folded_ref, x_ref, gates_ref, keep_ref, pool_ref, list_ref = refs[:6]
    neighbours_ref, valid_ref, pairing_ref, cot_ref, stage, sems, *totals = refs[6:]
    core = lax.axis_index("chan")
    first = lax.axis_index("tile") * tiles
    small, (features_copy, list_copy, *waits) = split(
        copies(
            [neighbours_hbm, valid_hbm, pairing_hbm, features_hbm.at[0], neighbours_hbm] + [cot_hbm.at[k] for k in range(NEIGHBOURS)],
            [neighbours_ref, valid_ref, pairing_ref, x_ref, list_ref] + [cot_ref.at[k] for k in range(NEIGHBOURS)],
            sems,
        ),
        3,
    )
    pool_ref[...] = coarse_weights((PAD, PIXELS), 1)
    pool = coarse_weights((PIXELS, PAD), 0)
    for total in totals:
        total[...] = jnp.zeros_like(total)
    for copy in small:
        copy.wait()
    keep = [valid_row(valid_ref, a, core, half) for a in range(tiles)]
    columns = [jnp.broadcast_to(column_of(row), (half, half)) for row in keep]
    for j in range(partners):
        weight = gate(pairing_ref, j, partners)
        gates_ref[j] = jnp.full(gates_ref.shape[1:], weight, jnp.float32)
        for a in range(tiles):
            keep_ref[j, a * half : (a + 1) * half] = columns[a] * weight
    for k, copy in enumerate(waits):
        copy.wait()
        stage[k % STAGES] = cot_ref[k].astype(jnp.float32).reshape(LEVELS * tiles, half)
        for a in range(tiles):
            w = relative(neighbours_ref, a, k, first)
            totals[a][w, :LEVELS] += stage[k % STAGES, pl.ds(a, LEVELS, stride=tiles), :]
    for a in range(tiles):
        for w in range(SPAN):
            coarse = totals[a][w, PIXELS:].astype(jnp.bfloat16)
            spread = jnp.dot(pool, coarse, preferred_element_type=jnp.float32)
            folded_ref[fold_rows(a, w)] = ((totals[a][w, :PIXELS] + spread) * keep[a]).astype(jnp.bfloat16)
    features_copy.wait()
    list_copy.wait()
    _, there = halves(core, half)
    for a in range(tiles):
        folded_ref[query_rows(tiles, half, a)] = x_ref[a, there, :]


def split(items, count):
    return items[:count], items[count:]


def fold_rows(a, w):
    start = (a * SPAN + w) * PIXELS
    return slice(start, start + PIXELS)


def query_rows(tiles, half, a):
    start = tiles * SPAN * PIXELS + a * half
    return slice(start, start + half)


def fold(partners, neighbours, valid, pairing, cotangent, features):
    half = cotangent.shape[-1]
    _, tiles, pixels, channels = features.shape
    return call(
        functools.partial(fold_kernel, tiles, half, partners),
        "fold",
        (
            shape_of((tiles * SPAN * PIXELS + tiles * half, half)),
            shape_of((tiles, pixels, channels)),
            shape_of((partners, 8, channels), jnp.float32),
            shape_of((partners, tiles * half, channels), jnp.float32),
            shape_of((PAD, PIXELS)),
            shape_of(neighbours.shape, jnp.int32),
        ),
        [HBM] * 5,
        (VMEM,) * 6,
        [
            pltpu.SMEM(neighbours.shape, jnp.int32),
            pltpu.VMEM(valid.shape, jnp.int32),
            pltpu.SMEM(pairing.shape, jnp.int32),
            pltpu.VMEM(cotangent.shape, jnp.bfloat16),
            pltpu.VMEM((STAGES, LEVELS * tiles, half), jnp.float32),
            pltpu.SemaphoreType.DMA((5 + NEIGHBOURS,)),
        ]
        + [pltpu.VMEM((SPAN, WIDE, half), jnp.float32)] * tiles,
        10,
    )(*in_hbm(neighbours, valid, pairing, cotangent, features))


def halves(core, half):
    here = pl.ds(pl.multiple_of(core * half, half), half)
    there = pl.ds(pl.multiple_of((1 - core) * half, half), half)
    return here, there


def window_grad(tiles, slot, queries, folded_ref):
    users = [a for a in range(tiles) if 0 <= slot - a < SPAN]
    blocks = [folded_ref[fold_rows(a, slot - a)] for a in users]
    return jnp.dot(
        jnp.concatenate(blocks, axis=1),
        jnp.concatenate([queries[a] for a in users], axis=0),
        preferred_element_type=jnp.float32,
    )


def early_kernel(tiles, half, x_ref, mine_ref, part_ref):
    here, _ = halves(lax.axis_index("chan"), half)
    queries = [x_ref[a, here, :] for a in range(tiles)]
    for slot in range(3 * tiles):
        part_ref[slot] = window_grad(tiles, slot, queries, mine_ref)


def early(x, mine):
    tiles, pixels, channels = x.shape
    return call(
        functools.partial(early_kernel, tiles, mine.shape[1]),
        "early",
        shape_of((3 * tiles, pixels, channels), jnp.float32),
        [VMEM] * 2,
        VMEM,
        [],
        4,
    )(x, mine)


def keys_kernel(tiles, half, x_ref, part_ref, other_ref, own_ref, even_ref, odd_ref):
    _, there = halves(lax.axis_index("chan"), half)
    queries = [x_ref[a, there, :] for a in range(tiles)]

    def of_slot(slot):
        return part_ref[slot] + window_grad(tiles, slot, queries, other_ref)

    parity = lax.rem(lax.axis_index("tile"), 2)
    for a in range(tiles):
        below = of_slot(a).astype(jnp.bfloat16)
        above = of_slot(2 * tiles + a).astype(jnp.bfloat16)
        even_ref[a] = jnp.where(parity == 0, above, below)
        odd_ref[a] = jnp.where(parity == 0, below, above)
        own_ref[a] = of_slot(tiles + a)


def keys(x, part, other):
    tiles, half = x.shape[0], other.shape[1]
    return call(
        functools.partial(keys_kernel, tiles, half),
        "keys",
        (shape_of(x.shape, jnp.float32), shape_of(x.shape), shape_of(x.shape)),
        [VMEM] * 3,
        (VMEM,) * 3,
        [],
        4,
    )(x, part, other)


def returns_kernel(partners, gates_ref, own_ref, even_ref, odd_ref, *out_refs):
    tile, count = lax.axis_index("tile"), lax.axis_size("tile")
    parity = lax.rem(tile, 2)
    has_even = jnp.logical_or(parity == 1, tile + 1 < count)
    has_odd = jnp.logical_or(jnp.logical_and(parity == 0, tile > 0), jnp.logical_and(parity == 1, tile + 1 < count))
    tiles, pixels, _ = own_ref.shape
    for a in range(tiles):
        total = own_ref[a]
        total = total + jnp.where(has_even, even_ref[a].astype(jnp.float32), 0.0)
        total = total + jnp.where(has_odd, odd_ref[a].astype(jnp.float32), 0.0)
        for j in range(partners):
            out_refs[j][a * pixels : (a + 1) * pixels] = (total * gates_ref[j, :1]).astype(jnp.bfloat16)
    for j in range(partners):
        out_refs[j][tiles * pixels :] = jnp.zeros((MARGIN, out_refs[j].shape[1]), jnp.bfloat16)


def returns(partners, gates, own, even, odd):
    tiles, pixels, channels = own.shape
    return call(
        functools.partial(returns_kernel, partners),
        "returns",
        (shape_of((tiles * pixels + MARGIN, channels)),) * partners,
        [VMEM] * 4,
        (VMEM,) * partners,
        [],
        3,
    )(gates, own, even, odd)


def join(mine, other):
    core = lax.axis_index("chan")
    return jnp.concatenate([jnp.where(core == 0, mine, other), jnp.where(core == 0, other, mine)], axis=-1)


def multiply(left, right, contract):
    return lax.dot_general(left, right, ((contract[:1], contract[1:]), ((), ())), preferred_element_type=jnp.float32)


def query_grads(gates_ref, folded_ref, other_ref, tiles, partners, level_of, slots):
    grads = []
    for a in range(tiles):
        grad = None
        for j in range(partners):
            term = None
            for slot in slots:
                if 0 <= slot - a < SPAN:
                    rows = fold_rows(a, slot - a)
                    both = jnp.concatenate([folded_ref[rows], other_ref[rows]], axis=1)
                    part = multiply(both, level_of(j, slot), (0, 0))
                    term = part if term is None else term + part
            term = term * gates_ref[j, :1]
            grad = term if grad is None else grad + term
        grads.append(grad)
    return grads


def ready_kernel(tiles, half, partners, gates_ref, keep_ref, x_ref, folded_ref, other_ref, *refs):
    same, (queries_ref, grad_ref) = refs[:partners], refs[partners:]
    here, _ = halves(lax.axis_index("chan"), half)
    mine = jnp.concatenate([x_ref[a, here, :] for a in range(tiles)], axis=0).astype(jnp.float32)
    other = jnp.concatenate([other_ref[query_rows(tiles, half, a)] for a in range(tiles)], axis=0).astype(jnp.float32)
    for j in range(partners):
        queries_ref[j] = join(mine * keep_ref[j], other * keep_ref[j]).T.astype(jnp.bfloat16)
    slots = range(tiles, 2 * tiles)
    grads = query_grads(
        gates_ref, folded_ref, other_ref, tiles, partners, lambda j, slot: same[j][slot - tiles], slots
    )
    for a in range(tiles):
        grad_ref[a] = grads[a]


def ready(partners, gates, keep, x, folded, other, same):
    tiles, pixels, channels = x.shape
    return call(
        functools.partial(ready_kernel, tiles, pixels // 2, partners),
        "ready",
        (shape_of((partners, 2 * channels, tiles * pixels // 2)), shape_of(x.shape, jnp.float32)),
        [VMEM] * (5 + len(same)),
        (VMEM,) * 2,
        [],
        6,
    )(gates, keep, x, folded, other, *same)


def sides_kernel(tiles, half, partners, gates_ref, folded_ref, other_ref, part_ref, *refs):
    inputs, (grad_ref, levels) = refs[: 2 * partners], refs[2 * partners :]
    here, there = halves(lax.axis_index("chan"), half)
    for j in range(partners):
        for part, base in enumerate(side_bases(tiles)):
            levels[j, pl.ds(base, tiles)] = inputs[2 * j + part][...]
    slots = [slot for slot in range(3 * tiles) if not tiles <= slot < 2 * tiles]
    grads = query_grads(
        gates_ref, folded_ref, other_ref, tiles, partners, lambda j, slot: levels[j, slot], slots
    )
    for a in range(tiles):
        grad = part_ref[a] + grads[a]
        grad_ref[a, here, :] = grad[:half]
        grad_ref[a, there, :] = grad[half:]


def sides(partners, gates, folded, other, part, windows):
    tiles, pixels, channels = windows[0].shape
    return call(
        functools.partial(sides_kernel, tiles, pixels // 2, partners),
        "sides",
        shape_of(windows[0].shape, jnp.float32),
        [VMEM] * (4 + len(windows)),
        VMEM,
        [pltpu.VMEM((partners, 3 * tiles, pixels, channels), jnp.bfloat16)],
        6,
    )(gates, folded, other, part, *windows)


def near_kernel(tiles, partners, queries_ref, pool_ref, *refs):
    same, (fine_ref, coarse_ref) = refs[: 2 * partners], refs[2 * partners :]
    pool = pool_ref[...]
    for s in range(tiles):
        fine, coarse = None, None
        for j in range(partners):
            level = join(same[2 * j][s], same[2 * j + 1][s])
            cells = jnp.dot(pool, level, preferred_element_type=jnp.float32).astype(jnp.bfloat16)
            fine_term = multiply(level, queries_ref[j], (1, 0))
            coarse_term = multiply(cells, queries_ref[j], (1, 0))
            fine = fine_term if fine is None else fine + fine_term
            coarse = coarse_term if coarse is None else coarse + coarse_term
        fine_ref[s] = fine
        coarse_ref[s] = coarse


def near(partners, queries, pool, same):
    tiles, pixels, _ = same[0].shape
    return call(
        functools.partial(near_kernel, tiles, partners),
        "near",
        (
            shape_of((tiles, pixels, tiles * pixels // 2), jnp.float32),
            shape_of((tiles, PAD, tiles * pixels // 2), jnp.float32),
        ),
        [VMEM] * (2 + len(same)),
        (VMEM,) * 2,
        [],
        6,
    )(queries, pool, *same)


def tables_kernel(tiles, partners, queries_ref, pool_ref, near_fine, near_coarse, *refs):
    inputs, (fine_table, coarse_table, levels, cells) = refs[: 4 * partners], refs[4 * partners :]
    fine_table[tiles : 2 * tiles] = near_fine[...]
    coarse_table[tiles : 2 * tiles] = near_coarse[...]
    pool = pool_ref[...]
    for j in range(partners):
        for part in range(2):
            for a in range(tiles):
                level = join(inputs[4 * j + part][a], inputs[4 * j + 2 + part][a])
                at = part * tiles + a
                levels[j, at * PIXELS : (at + 1) * PIXELS] = level
                cells[j, at * PAD : (at + 1) * PAD] = jnp.dot(
                    pool, level, preferred_element_type=jnp.float32
                ).astype(jnp.bfloat16)
    for keys_at, table in ((levels, fine_table), (cells, coarse_table)):
        scores = multiply(keys_at[0], queries_ref[0], (1, 0))
        for j in range(1, partners):
            scores = scores + multiply(keys_at[j], queries_ref[j], (1, 0))
        scores = scores.reshape(2, tiles, table.shape[1], table.shape[2])
        for part, base in enumerate(side_bases(tiles)):
            table[pl.ds(base, tiles)] = scores[part]


def tables(partners, queries, pool, fine, coarse, beside):
    tiles, pixels, channels = beside[0].shape
    return call(
        functools.partial(tables_kernel, tiles, partners),
        "tables",
        tuple(shape_of((3 * tiles,) + near.shape[1:], jnp.float32) for near in (fine, coarse)),
        [VMEM] * (4 + len(beside)),
        (VMEM,) * 2,
        [
            pltpu.VMEM((partners, 2 * tiles * pixels, 2 * channels), jnp.bfloat16),
            pltpu.VMEM((partners, 2 * tiles * PAD, 2 * channels), jnp.bfloat16),
        ],
        7,
    )(queries, pool, fine, coarse, *beside)


def volume_kernel(tiles, half, partners, list_ref, part_ref, fine_table, coarse_table, *refs):
    returned, (volume_hbm, grad_hbm, stage, volume_ref, grad_ref, sems) = refs[:partners], refs[partners:]
    first = lax.axis_index("tile") * tiles
    listed = list_ref[...]
    pixels, channels = grad_ref.shape[1:]
    for a in range(tiles):
        summed = part_ref[a]
        for j in range(partners):
            summed = summed + returned[j][a * pixels : (a + 1) * pixels].astype(jnp.float32)
        grad_ref[a] = summed
    waits = [pltpu.make_async_copy(grad_ref, grad_hbm.at[0], sems.at[0])]
    waits[0].start()
    for i_part, (entries, start, size) in enumerate(entry_pairs(tiles)):
        for i, k in enumerate(entries):
            for a in range(tiles):
                slot = relative(listed, a, k, first) + a
                lanes = slice(a * half, (a + 1) * half)
                base = i * LEVELS * tiles + a
                stage[pl.ds(base, PIXELS, stride=tiles), :] = fine_table[slot, :, lanes]
                stage[pl.ds(base + PIXELS * tiles, COARSE, stride=tiles), :] = coarse_table[slot, :COARSE, lanes]
        rows = pl.ds(start, size)
        volume_ref[rows, :] = stage[:size].astype(jnp.bfloat16)
        copy = pltpu.make_async_copy(volume_ref.at[rows], volume_hbm.at[rows], sems.at[1 + i_part])
        copy.start()
        waits.append(copy)
    for copy in waits:
        copy.wait()


def volumes(partners, neighbours, grad, fine, coarse, returned):
    tiles, pixels, _ = grad.shape
    half = pixels // 2
    rows = NEIGHBOURS * LEVELS * tiles
    return call(
        functools.partial(volume_kernel, tiles, half, partners),
        "volume",
        (shape_of((rows, half)), shape_of((1,) + grad.shape, jnp.float32)),
        [VMEM] * (4 + len(returned)),
        (HBM, HBM),
        [
            pltpu.VMEM((2 * LEVELS * tiles, half), jnp.float32),
            pltpu.VMEM((rows, half), jnp.bfloat16),
            pltpu.VMEM(grad.shape, jnp.float32),
            pltpu.SemaphoreType.DMA((1 + (NEIGHBOURS + 1) // 2,)),
        ],
        8,
    )(neighbours, grad, fine, coarse, *returned)


def after(value, earlier):
    return lax.optimization_barrier((value, earlier))[0]


def local(features, neighbours, pairing, valid_tiles, cotangent):
    count = lax.axis_size("tile")
    cores = lax.axis_size("chan")
    links = frame_links(lax.axis_size("frame"))
    partners = len(links)
    tiles, half = cotangent.shape[1:3]
    swap = [(c, (c + 1) % cores) for c in range(cores)]
    evens, odds = even_pairs(count), odd_pairs(count, cores)

    def over_even(z):
        return lax.ppermute(z, "tile", evens)

    def over_odd(z):
        return lax.ppermute(z, ("tile", "chan"), odds)

    def over_cores(z):
        return lax.ppermute(z, "chan", swap)

    upstream = jnp.transpose(cotangent[0], (2, 0, 1)).reshape(NEIGHBOURS, LEVELS * tiles // 8, 8, half)
    folded, x, gates, keep, pool, listed = fold(partners, neighbours, valid_tiles, pairing, upstream, features)
    other = over_cores(folded)
    arrived = [lax.ppermute(x, "frame", ahead) for ahead, _ in links]
    own, to_even, to_odd = keys(x, early(x, folded), other)
    arrived = [after(y, own) for y in arrived]
    beside = [(over_even(y), over_odd(y)) for y in arrived]
    from_odd = over_odd(to_odd)
    from_even = after(over_even(to_even), from_odd)
    sent = returns(partners, gates, own, from_even, from_odd)
    returned = [lax.ppermute(z, "frame", back) for z, (_, back) in zip(sent, links, strict=True)]
    queries, part = ready(partners, gates, keep, x, folded, other, [after(y, sent[0]) for y in arrived])
    same, mine, exchanged = [], [], []
    for y, (even, odd) in zip(arrived, beside, strict=True):
        even, odd = after(even, part), after(odd, part)
        same += [after(y, odd), after(over_cores(y), odd)]
        mine += [even, odd]
        exchanged += [even, odd, over_cores(even), over_cores(odd)]
    grad = sides(partners, gates, folded, other, part, mine)
    fine, coarse = near(partners, queries, pool, [after(z, grad) for z in same])
    exchanged = [after(after(z, grad), fine) for z in exchanged]
    fine, coarse = tables(partners, queries, pool, fine, coarse, exchanged)
    returned = [after(z, fine) for z in returned]
    volume, feature_grad = volumes(partners, listed, grad, fine, coarse, returned)
    volume = jnp.transpose(volume.reshape(NEIGHBOURS * LEVELS, tiles, half), (1, 2, 0))
    return volume[None], feature_grad


def solution(mesh):
    return jax.shard_map(
        local,
        mesh=mesh,
        in_specs=(
            P(("clip", "frame"), "tile", None, "chan"),
            P(("clip", "tile"), None),
            P(("clip", "frame"), None),
            P(("clip", "tile"), None),
            P(("clip", "frame"), "tile", "chan", None),
        ),
        out_specs=(
            P(("clip", "frame"), "tile", "chan", None),
            P(("clip", "frame"), "tile", None, "chan"),
        ),
        check_vma=False,
    )
```

```python
import functools

import jax
import jax.numpy as jnp
from jax import lax
from jax.experimental import pallas as pl
from jax.experimental.pallas import tpu as pltpu
from jax.sharding import PartitionSpec as P

CHANNELS = 256
SIDE = 16
PIXELS = 256
LEVELS = 340
NEIGHBOURS = 9
REACH = 2
SPAN = 2 * REACH + 1
COARSE = LEVELS - PIXELS
MARGIN = 16
STAGES = 9
PAD = 128
WIDE = PIXELS + PAD

VMEM = pl.BlockSpec(memory_space=pltpu.VMEM)
HBM = pl.BlockSpec(memory_space=pltpu.HBM)


def even_pairs(count):
    pairs = []
    for i in range(0, count - 1, 2):
        pairs += [(i, i + 1), (i + 1, i)]
    if count % 2:
        pairs.append((count - 1, count - 1))
    return pairs


def odd_pairs(count, cores):
    pairs, paired = [], set()
    for i in range(1, count - 1, 2):
        paired |= {i, i + 1}
        for c in range(cores):
            pairs += [(i * cores + c, (i + 1) * cores + c), ((i + 1) * cores + c, i * cores + c)]
    for i in range(count):
        if i not in paired:
            pairs += [(i * cores + c, i * cores + (c + 1) % cores) for c in range(cores)]
    return pairs


def frame_links(count):
    if count == 2:
        swap = [(0, 1), (1, 0)]
        return [(swap, swap)]
    onward = [(i, i + 1) for i in range(count - 1)]
    back = [(i + 1, i) for i in range(count - 1)]
    return [(onward, back), (back, onward)]


def coarse_weights(shape, pixel_axis):
    pixel = lax.broadcasted_iota(jnp.int32, shape, pixel_axis)
    cell = lax.broadcasted_iota(jnp.int32, shape, 1 - pixel_axis)
    row, column = lax.shift_right_logical(pixel, 4), jnp.bitwise_and(pixel, SIDE - 1)
    table = jnp.zeros(shape, jnp.float32)
    base = 0
    for level, across in ((1, 8), (2, 4), (3, 2)):
        target = base + lax.shift_right_logical(row, level) * across + lax.shift_right_logical(column, level)
        table = jnp.where(cell == target, 0.25**level, table)
        base += across * across
    return table.astype(jnp.bfloat16)


def column_of(row):
    n = row.shape[1]
    diagonal = lax.broadcasted_iota(jnp.int32, (n, n), 0) == lax.broadcasted_iota(jnp.int32, (n, n), 1)
    return jnp.sum(jnp.where(diagonal, row, 0.0), axis=1, keepdims=True)


def valid_row(valid_ref, a, core, half):
    row = valid_ref[a : a + 1, :].astype(jnp.float32)
    return jnp.where(core == 0, row[:, :half], row[:, half:])


def relative(neighbours_ref, a, k, first):
    return neighbours_ref[a, k] - (first + a) + REACH


def gate(pairing_ref, j, partners):
    if partners == 1:
        column = 1 - lax.axis_index("frame")
    else:
        column = j
    return pairing_ref[0, column].astype(jnp.float32) / 16.0


def entry_pairs(tiles):
    rows = LEVELS * tiles
    for k in range(0, NEIGHBOURS, 2):
        entries = range(k, min(k + 2, NEIGHBOURS))
        yield entries, k * rows, len(entries) * rows


def in_hbm(*arrays):
    return [pltpu.with_memory_space_constraint(z, pltpu.HBM) for z in arrays]


def copies(sources, targets, sems):
    started = [pltpu.make_async_copy(s, t, sems.at[i]) for i, (s, t) in enumerate(zip(sources, targets, strict=True))]
    for copy in started:
        copy.start()
    return started


def side_bases(tiles):
    parity = lax.rem(lax.axis_index("tile"), 2)
    return (1 - parity) * 2 * tiles, parity * 2 * tiles


def shape_of(shape, dtype=jnp.bfloat16):
    return jax.ShapeDtypeStruct(shape, dtype)


def call(kernel, name, outs, in_specs, out_specs, scratch, vmem_mib):
    return pl.pallas_call(
        kernel,
        out_shape=outs,
        in_specs=in_specs,
        out_specs=out_specs,
        scratch_shapes=scratch,
        compiler_params=pltpu.CompilerParams(vmem_limit_bytes=vmem_mib * 2**20),
        name=name,
    )


def fold_kernel(tiles, half, partners, neighbours_hbm, valid_hbm, pairing_hbm, cot_hbm, features_hbm, *refs):
    folded_ref, x_ref, gates_ref, keep_ref, pool_ref, list_ref = refs[:6]
    neighbours_ref, valid_ref, pairing_ref, cot_ref, stage, sems, *totals = refs[6:]
    core = lax.axis_index("chan")
    first = lax.axis_index("tile") * tiles
    small, (*waits, features_copy, list_copy) = split(
        copies(
            [neighbours_hbm, valid_hbm, pairing_hbm]
            + [cot_hbm.at[k] for k in range(NEIGHBOURS)]
            + [features_hbm.at[0], neighbours_hbm],
            [neighbours_ref, valid_ref, pairing_ref] + [cot_ref.at[k] for k in range(NEIGHBOURS)] + [x_ref, list_ref],
            sems,
        ),
        3,
    )
    pool_ref[...] = coarse_weights((PAD, PIXELS), 1)
    pool = coarse_weights((PIXELS, PAD), 0)
    for total in totals:
        total[...] = jnp.zeros_like(total)
    for copy in small:
        copy.wait()
    keep = [valid_row(valid_ref, a, core, half) for a in range(tiles)]
    columns = [jnp.broadcast_to(column_of(row), (half, half)) for row in keep]
    for j in range(partners):
        weight = gate(pairing_ref, j, partners)
        gates_ref[j] = jnp.full(gates_ref.shape[1:], weight, jnp.float32)
        for a in range(tiles):
            keep_ref[j, a * half : (a + 1) * half] = columns[a] * weight
    for k, copy in enumerate(waits):
        copy.wait()
        stage[k % STAGES] = cot_ref[k].astype(jnp.float32).reshape(LEVELS * tiles, half)
        for a in range(tiles):
            w = relative(neighbours_ref, a, k, first)
            totals[a][w, :LEVELS] += stage[k % STAGES, pl.ds(a, LEVELS, stride=tiles), :]
    for a in range(tiles):
        for w in range(SPAN):
            coarse = totals[a][w, PIXELS:].astype(jnp.bfloat16)
            spread = jnp.dot(pool, coarse, preferred_element_type=jnp.float32)
            folded_ref[fold_rows(a, w)] = ((totals[a][w, :PIXELS] + spread) * keep[a]).astype(jnp.bfloat16)
    features_copy.wait()
    list_copy.wait()


def split(items, count):
    return items[:count], items[count:]


def fold_rows(a, w):
    start = (a * SPAN + w) * PIXELS
    return slice(start, start + PIXELS)


def fold(partners, neighbours, valid, pairing, cotangent, features):
    half = cotangent.shape[-1]
    _, tiles, pixels, channels = features.shape
    return call(
        functools.partial(fold_kernel, tiles, half, partners),
        "fold",
        (
            shape_of((tiles * SPAN * PIXELS, half)),
            shape_of((tiles, pixels, channels)),
            shape_of((partners, 8, channels), jnp.float32),
            shape_of((partners, tiles * half, channels), jnp.float32),
            shape_of((PAD, PIXELS)),
            shape_of(neighbours.shape, jnp.int32),
        ),
        [HBM] * 5,
        (VMEM,) * 6,
        [
            pltpu.SMEM(neighbours.shape, jnp.int32),
            pltpu.VMEM(valid.shape, jnp.int32),
            pltpu.SMEM(pairing.shape, jnp.int32),
            pltpu.VMEM(cotangent.shape, jnp.bfloat16),
            pltpu.VMEM((STAGES, LEVELS * tiles, half), jnp.float32),
            pltpu.SemaphoreType.DMA((5 + NEIGHBOURS,)),
        ]
        + [pltpu.VMEM((SPAN, WIDE, half), jnp.float32)] * tiles,
        10,
    )(*in_hbm(neighbours, valid, pairing, cotangent, features))


def halves(core, half):
    here = pl.ds(pl.multiple_of(core * half, half), half)
    there = pl.ds(pl.multiple_of((1 - core) * half, half), half)
    return here, there


def window_grad(tiles, slot, queries, folded_ref):
    users = [a for a in range(tiles) if 0 <= slot - a < SPAN]
    blocks = [folded_ref[fold_rows(a, slot - a)] for a in users]
    return jnp.dot(
        jnp.concatenate(blocks, axis=1),
        jnp.concatenate([queries[a] for a in users], axis=0),
        preferred_element_type=jnp.float32,
    )


def early_kernel(tiles, half, x_ref, mine_ref, part_ref):
    here, _ = halves(lax.axis_index("chan"), half)
    queries = [x_ref[a, here, :] for a in range(tiles)]
    for slot in range(3 * tiles):
        part_ref[slot] = window_grad(tiles, slot, queries, mine_ref)


def early(x, mine):
    tiles, pixels, channels = x.shape
    return call(
        functools.partial(early_kernel, tiles, mine.shape[1]),
        "early",
        shape_of((3 * tiles, pixels, channels), jnp.float32),
        [VMEM] * 2,
        VMEM,
        [],
        4,
    )(x, mine)


def keys_kernel(tiles, half, x_ref, part_ref, other_ref, own_ref, even_ref, odd_ref):
    _, there = halves(lax.axis_index("chan"), half)
    queries = [x_ref[a, there, :] for a in range(tiles)]

    def of_slot(slot):
        return part_ref[slot] + window_grad(tiles, slot, queries, other_ref)

    parity = lax.rem(lax.axis_index("tile"), 2)
    for a in range(tiles):
        below = of_slot(a).astype(jnp.bfloat16)
        above = of_slot(2 * tiles + a).astype(jnp.bfloat16)
        even_ref[a] = jnp.where(parity == 0, above, below)
        odd_ref[a] = jnp.where(parity == 0, below, above)
        own_ref[a] = of_slot(tiles + a)


def keys(x, part, other):
    tiles, half = x.shape[0], other.shape[1]
    return call(
        functools.partial(keys_kernel, tiles, half),
        "keys",
        (shape_of(x.shape, jnp.float32), shape_of(x.shape), shape_of(x.shape)),
        [VMEM] * 3,
        (VMEM,) * 3,
        [],
        4,
    )(x, part, other)


def returns_kernel(partners, gates_ref, own_ref, even_ref, odd_ref, *out_refs):
    tile, count = lax.axis_index("tile"), lax.axis_size("tile")
    parity = lax.rem(tile, 2)
    has_even = jnp.logical_or(parity == 1, tile + 1 < count)
    has_odd = jnp.logical_or(jnp.logical_and(parity == 0, tile > 0), jnp.logical_and(parity == 1, tile + 1 < count))
    tiles, pixels, _ = own_ref.shape
    for a in range(tiles):
        total = own_ref[a]
        total = total + jnp.where(has_even, even_ref[a].astype(jnp.float32), 0.0)
        total = total + jnp.where(has_odd, odd_ref[a].astype(jnp.float32), 0.0)
        for j in range(partners):
            out_refs[j][a * pixels : (a + 1) * pixels] = (total * gates_ref[j, :1]).astype(jnp.bfloat16)
    for j in range(partners):
        out_refs[j][tiles * pixels :] = jnp.zeros((MARGIN, out_refs[j].shape[1]), jnp.bfloat16)


def returns(partners, gates, own, even, odd):
    tiles, pixels, channels = own.shape
    return call(
        functools.partial(returns_kernel, partners),
        "returns",
        (shape_of((tiles * pixels + MARGIN, channels)),) * partners,
        [VMEM] * 4,
        (VMEM,) * partners,
        [],
        3,
    )(gates, own, even, odd)


def join(mine, other):
    core = lax.axis_index("chan")
    return jnp.concatenate([jnp.where(core == 0, mine, other), jnp.where(core == 0, other, mine)], axis=-1)


def multiply(left, right, contract):
    return lax.dot_general(left, right, ((contract[:1], contract[1:]), ((), ())), preferred_element_type=jnp.float32)


def query_grads(gates_ref, folded_ref, other_ref, tiles, partners, level_of, slots):
    grads = []
    for a in range(tiles):
        grad = None
        for j in range(partners):
            term = None
            for slot in slots:
                if 0 <= slot - a < SPAN:
                    rows = fold_rows(a, slot - a)
                    both = jnp.concatenate([folded_ref[rows], other_ref[rows]], axis=1)
                    part = multiply(both, level_of(j, slot), (0, 0))
                    term = part if term is None else term + part
            term = term * gates_ref[j, :1]
            grad = term if grad is None else grad + term
        grads.append(grad)
    return grads


def ready_kernel(tiles, half, partners, gates_ref, keep_ref, x_ref, xo_ref, folded_ref, other_ref, *refs):
    same, (queries_ref, grad_ref) = refs[:partners], refs[partners:]
    here, _ = halves(lax.axis_index("chan"), half)
    mine = jnp.concatenate([x_ref[a, here, :] for a in range(tiles)], axis=0).astype(jnp.float32)
    other = jnp.concatenate([xo_ref[a, here, :] for a in range(tiles)], axis=0).astype(jnp.float32)
    for j in range(partners):
        queries_ref[j] = join(mine * keep_ref[j], other * keep_ref[j]).T.astype(jnp.bfloat16)
    slots = range(tiles, 2 * tiles)
    grads = query_grads(
        gates_ref, folded_ref, other_ref, tiles, partners, lambda j, slot: same[j][slot - tiles], slots
    )
    for a in range(tiles):
        grad_ref[a] = grads[a]


def ready(partners, gates, keep, x, xo, folded, other, same):
    tiles, pixels, channels = x.shape
    return call(
        functools.partial(ready_kernel, tiles, pixels // 2, partners),
        "ready",
        (shape_of((partners, 2 * channels, tiles * pixels // 2)), shape_of(x.shape, jnp.float32)),
        [VMEM] * (6 + len(same)),
        (VMEM,) * 2,
        [],
        6,
    )(gates, keep, x, xo, folded, other, *same)


def sides_kernel(tiles, half, partners, gates_ref, folded_ref, other_ref, part_ref, *refs):
    inputs, (grad_ref, levels) = refs[: 2 * partners], refs[2 * partners :]
    here, there = halves(lax.axis_index("chan"), half)
    for j in range(partners):
        for part, base in enumerate(side_bases(tiles)):
            levels[j, pl.ds(base, tiles)] = inputs[2 * j + part][...]
    slots = [slot for slot in range(3 * tiles) if not tiles <= slot < 2 * tiles]
    grads = query_grads(
        gates_ref, folded_ref, other_ref, tiles, partners, lambda j, slot: levels[j, slot], slots
    )
    for a in range(tiles):
        grad = part_ref[a] + grads[a]
        grad_ref[a, here, :] = grad[:half]
        grad_ref[a, there, :] = grad[half:]


def sides(partners, gates, folded, other, part, windows):
    tiles, pixels, channels = windows[0].shape
    return call(
        functools.partial(sides_kernel, tiles, pixels // 2, partners),
        "sides",
        shape_of(windows[0].shape, jnp.float32),
        [VMEM] * (4 + len(windows)),
        VMEM,
        [pltpu.VMEM((partners, 3 * tiles, pixels, channels), jnp.bfloat16)],
        6,
    )(gates, folded, other, part, *windows)


def near_kernel(tiles, partners, queries_ref, pool_ref, *refs):
    same, (fine_ref, coarse_ref) = refs[: 2 * partners], refs[2 * partners :]
    pool = pool_ref[...]
    for s in range(tiles):
        fine, coarse = None, None
        for j in range(partners):
            level = join(same[2 * j][s], same[2 * j + 1][s])
            cells = jnp.dot(pool, level, preferred_element_type=jnp.float32).astype(jnp.bfloat16)
            fine_term = multiply(level, queries_ref[j], (1, 0))
            coarse_term = multiply(cells, queries_ref[j], (1, 0))
            fine = fine_term if fine is None else fine + fine_term
            coarse = coarse_term if coarse is None else coarse + coarse_term
        fine_ref[s] = fine
        coarse_ref[s] = coarse


def near(partners, queries, pool, same):
    tiles, pixels, _ = same[0].shape
    return call(
        functools.partial(near_kernel, tiles, partners),
        "near",
        (
            shape_of((tiles, pixels, tiles * pixels // 2), jnp.float32),
            shape_of((tiles, PAD, tiles * pixels // 2), jnp.float32),
        ),
        [VMEM] * (2 + len(same)),
        (VMEM,) * 2,
        [],
        6,
    )(queries, pool, *same)


def tables_kernel(tiles, partners, queries_ref, pool_ref, near_fine, near_coarse, *refs):
    inputs, (fine_table, coarse_table, levels, cells) = refs[: 4 * partners], refs[4 * partners :]
    fine_table[tiles : 2 * tiles] = near_fine[...]
    coarse_table[tiles : 2 * tiles] = near_coarse[...]
    pool = pool_ref[...]
    for j in range(partners):
        for part in range(2):
            for a in range(tiles):
                level = join(inputs[4 * j + part][a], inputs[4 * j + 2 + part][a])
                at = part * tiles + a
                levels[j, at * PIXELS : (at + 1) * PIXELS] = level
                cells[j, at * PAD : (at + 1) * PAD] = jnp.dot(
                    pool, level, preferred_element_type=jnp.float32
                ).astype(jnp.bfloat16)
    for keys_at, table in ((levels, fine_table), (cells, coarse_table)):
        scores = multiply(keys_at[0], queries_ref[0], (1, 0))
        for j in range(1, partners):
            scores = scores + multiply(keys_at[j], queries_ref[j], (1, 0))
        scores = scores.reshape(2, tiles, table.shape[1], table.shape[2])
        for part, base in enumerate(side_bases(tiles)):
            table[pl.ds(base, tiles)] = scores[part]


def tables(partners, queries, pool, fine, coarse, beside):
    tiles, pixels, channels = beside[0].shape
    return call(
        functools.partial(tables_kernel, tiles, partners),
        "tables",
        tuple(shape_of((3 * tiles,) + near.shape[1:], jnp.float32) for near in (fine, coarse)),
        [VMEM] * (4 + len(beside)),
        (VMEM,) * 2,
        [
            pltpu.VMEM((partners, 2 * tiles * pixels, 2 * channels), jnp.bfloat16),
            pltpu.VMEM((partners, 2 * tiles * PAD, 2 * channels), jnp.bfloat16),
        ],
        7,
    )(queries, pool, fine, coarse, *beside)


def volume_kernel(tiles, half, partners, list_ref, part_ref, fine_table, coarse_table, *refs):
    returned, (volume_hbm, grad_hbm, stage, volume_ref, grad_ref, sems) = refs[:partners], refs[partners:]
    first = lax.axis_index("tile") * tiles
    listed = list_ref[...]
    pixels, channels = grad_ref.shape[1:]
    for a in range(tiles):
        summed = part_ref[a]
        for j in range(partners):
            summed = summed + returned[j][a * pixels : (a + 1) * pixels].astype(jnp.float32)
        grad_ref[a] = summed
    waits = [pltpu.make_async_copy(grad_ref, grad_hbm.at[0], sems.at[0])]
    waits[0].start()
    for i_part, (entries, start, size) in enumerate(entry_pairs(tiles)):
        for i, k in enumerate(entries):
            for a in range(tiles):
                slot = relative(listed, a, k, first) + a
                lanes = slice(a * half, (a + 1) * half)
                base = i * LEVELS * tiles + a
                stage[pl.ds(base, PIXELS, stride=tiles), :] = fine_table[slot, :, lanes]
                stage[pl.ds(base + PIXELS * tiles, COARSE, stride=tiles), :] = coarse_table[slot, :COARSE, lanes]
        rows = pl.ds(start, size)
        volume_ref[rows, :] = stage[:size].astype(jnp.bfloat16)
        copy = pltpu.make_async_copy(volume_ref.at[rows], volume_hbm.at[rows], sems.at[1 + i_part])
        copy.start()
        waits.append(copy)
    for copy in waits:
        copy.wait()


def volumes(partners, neighbours, grad, fine, coarse, returned):
    tiles, pixels, _ = grad.shape
    half = pixels // 2
    rows = NEIGHBOURS * LEVELS * tiles
    return call(
        functools.partial(volume_kernel, tiles, half, partners),
        "volume",
        (shape_of((rows, half)), shape_of((1,) + grad.shape, jnp.float32)),
        [VMEM] * (4 + len(returned)),
        (HBM, HBM),
        [
            pltpu.VMEM((2 * LEVELS * tiles, half), jnp.float32),
            pltpu.VMEM((rows, half), jnp.bfloat16),
            pltpu.VMEM(grad.shape, jnp.float32),
            pltpu.SemaphoreType.DMA((1 + (NEIGHBOURS + 1) // 2,)),
        ],
        8,
    )(neighbours, grad, fine, coarse, *returned)


def after(value, earlier):
    return lax.optimization_barrier((value, earlier))[0]


def local(features, neighbours, pairing, valid_tiles, cotangent):
    count = lax.axis_size("tile")
    cores = lax.axis_size("chan")
    links = frame_links(lax.axis_size("frame"))
    partners = len(links)
    tiles, half = cotangent.shape[1:3]
    swap = [(c, (c + 1) % cores) for c in range(cores)]
    evens, odds = even_pairs(count), odd_pairs(count, cores)

    def over_even(z):
        return lax.ppermute(z, "tile", evens)

    def over_odd(z):
        return lax.ppermute(z, ("tile", "chan"), odds)

    def over_cores(z):
        return lax.ppermute(z, "chan", swap)

    upstream = jnp.transpose(cotangent[0], (2, 0, 1)).reshape(NEIGHBOURS, LEVELS * tiles // 8, 8, half)
    folded, x, gates, keep, pool, listed = fold(partners, neighbours, valid_tiles, pairing, upstream, features)
    other = over_cores(folded)
    arrived = [lax.ppermute(x, "frame", ahead) for ahead, _ in links]
    own, to_even, to_odd = keys(x, early(x, folded), other)
    xo = over_cores(x)
    arrived = [after(y, own) for y in arrived]
    beside = [(over_even(y), over_odd(y)) for y in arrived]
    from_odd = over_odd(to_odd)
    from_even = after(over_even(to_even), from_odd)
    sent = returns(partners, gates, own, from_even, from_odd)
    returned = [lax.ppermute(z, "frame", back) for z, (_, back) in zip(sent, links, strict=True)]
    queries, part = ready(partners, gates, keep, x, xo, folded, other, [after(y, sent[0]) for y in arrived])
    same, mine, exchanged = [], [], []
    for y, (even, odd) in zip(arrived, beside, strict=True):
        even, odd = after(even, part), after(odd, part)
        same += [after(y, odd), after(over_cores(y), odd)]
        mine += [even, odd]
        exchanged += [even, odd, over_cores(even), over_cores(odd)]
    grad = sides(partners, gates, folded, other, part, mine)
    fine, coarse = near(partners, queries, pool, [after(z, grad) for z in same])
    exchanged = [after(after(z, grad), fine) for z in exchanged]
    fine, coarse = tables(partners, queries, pool, fine, coarse, exchanged)
    returned = [after(z, fine) for z in returned]
    volume, feature_grad = volumes(partners, listed, grad, fine, coarse, returned)
    volume = jnp.transpose(volume.reshape(NEIGHBOURS * LEVELS, tiles, half), (1, 2, 0))
    return volume[None], feature_grad


def solution(mesh):
    return jax.shard_map(
        local,
        mesh=mesh,
        in_specs=(
            P(("clip", "frame"), "tile", None, "chan"),
            P(("clip", "tile"), None),
            P(("clip", "frame"), None),
            P(("clip", "tile"), None),
            P(("clip", "frame"), "tile", "chan", None),
        ),
        out_specs=(
            P(("clip", "frame"), "tile", "chan", None),
            P(("clip", "frame"), "tile", None, "chan"),
        ),
        check_vma=False,
    )
```

```python
import functools

import jax
import jax.numpy as jnp
from jax import lax
from jax.experimental import pallas as pl
from jax.experimental.pallas import tpu as pltpu
from jax.sharding import PartitionSpec as P

CHANNELS = 256
SIDE = 16
PIXELS = 256
LEVELS = 340
NEIGHBOURS = 9
REACH = 2
SPAN = 2 * REACH + 1
COARSE = LEVELS - PIXELS
MARGIN = 16
STAGES = 9
PAD = 128
WIDE = PIXELS + PAD

VMEM = pl.BlockSpec(memory_space=pltpu.VMEM)
HBM = pl.BlockSpec(memory_space=pltpu.HBM)


def even_pairs(count):
    pairs = []
    for i in range(0, count - 1, 2):
        pairs += [(i, i + 1), (i + 1, i)]
    if count % 2:
        pairs.append((count - 1, count - 1))
    return pairs


def odd_pairs(count, cores):
    pairs, paired = [], set()
    for i in range(1, count - 1, 2):
        paired |= {i, i + 1}
        for c in range(cores):
            pairs += [(i * cores + c, (i + 1) * cores + c), ((i + 1) * cores + c, i * cores + c)]
    for i in range(count):
        if i not in paired:
            pairs += [(i * cores + c, i * cores + (c + 1) % cores) for c in range(cores)]
    return pairs


def frame_links(count):
    if count == 2:
        swap = [(0, 1), (1, 0)]
        return [(swap, swap)]
    onward = [(i, i + 1) for i in range(count - 1)]
    back = [(i + 1, i) for i in range(count - 1)]
    return [(onward, back), (back, onward)]


def coarse_weights(shape, pixel_axis):
    pixel = lax.broadcasted_iota(jnp.int32, shape, pixel_axis)
    cell = lax.broadcasted_iota(jnp.int32, shape, 1 - pixel_axis)
    row, column = lax.shift_right_logical(pixel, 4), jnp.bitwise_and(pixel, SIDE - 1)
    table = jnp.zeros(shape, jnp.float32)
    base = 0
    for level, across in ((1, 8), (2, 4), (3, 2)):
        target = base + lax.shift_right_logical(row, level) * across + lax.shift_right_logical(column, level)
        table = jnp.where(cell == target, 0.25**level, table)
        base += across * across
    return table.astype(jnp.bfloat16)


def column_of(row):
    n = row.shape[1]
    diagonal = lax.broadcasted_iota(jnp.int32, (n, n), 0) == lax.broadcasted_iota(jnp.int32, (n, n), 1)
    return jnp.sum(jnp.where(diagonal, row, 0.0), axis=1, keepdims=True)


def valid_row(valid_ref, a, core, half):
    row = valid_ref[a : a + 1, :].astype(jnp.float32)
    return jnp.where(core == 0, row[:, :half], row[:, half:])


def relative(neighbours_ref, a, k, first):
    return neighbours_ref[a, k] - (first + a) + REACH


def gate(pairing_ref, j, partners):
    if partners == 1:
        column = 1 - lax.axis_index("frame")
    else:
        column = j
    return pairing_ref[0, column].astype(jnp.float32) / 16.0


def entry_pairs(tiles):
    rows = LEVELS * tiles
    for k in range(0, NEIGHBOURS, 2):
        entries = range(k, min(k + 2, NEIGHBOURS))
        yield entries, k * rows, len(entries) * rows


def in_hbm(*arrays):
    return [pltpu.with_memory_space_constraint(z, pltpu.HBM) for z in arrays]


def copies(sources, targets, sems):
    started = [pltpu.make_async_copy(s, t, sems.at[i]) for i, (s, t) in enumerate(zip(sources, targets, strict=True))]
    for copy in started:
        copy.start()
    return started


def side_bases(tiles):
    parity = lax.rem(lax.axis_index("tile"), 2)
    return (1 - parity) * 2 * tiles, parity * 2 * tiles


def shape_of(shape, dtype=jnp.bfloat16):
    return jax.ShapeDtypeStruct(shape, dtype)


def call(kernel, name, outs, in_specs, out_specs, scratch, vmem_mib):
    return pl.pallas_call(
        kernel,
        out_shape=outs,
        in_specs=in_specs,
        out_specs=out_specs,
        scratch_shapes=scratch,
        compiler_params=pltpu.CompilerParams(vmem_limit_bytes=vmem_mib * 2**20),
        name=name,
    )


def fold_kernel(tiles, half, partners, neighbours_hbm, valid_hbm, pairing_hbm, cot_hbm, features_hbm, *refs):
    folded_ref, x_ref, gates_ref, keep_ref, pool_ref, list_ref = refs[:6]
    neighbours_ref, valid_ref, pairing_ref, cot_ref, stage, sems, *totals = refs[6:]
    core = lax.axis_index("chan")
    first = lax.axis_index("tile") * tiles
    small, (*waits, features_copy, list_copy) = split(
        copies(
            [neighbours_hbm, valid_hbm, pairing_hbm]
            + [cot_hbm.at[k] for k in range(NEIGHBOURS)]
            + [features_hbm.at[0], neighbours_hbm],
            [neighbours_ref, valid_ref, pairing_ref] + [cot_ref.at[k] for k in range(NEIGHBOURS)] + [x_ref, list_ref],
            sems,
        ),
        3,
    )
    pool_ref[...] = coarse_weights((PAD, PIXELS), 1)
    pool = coarse_weights((PIXELS, PAD), 0)
    for total in totals:
        total[...] = jnp.zeros_like(total)
    for copy in small:
        copy.wait()
    keep = [valid_row(valid_ref, a, core, half) for a in range(tiles)]
    columns = [jnp.broadcast_to(column_of(row), (half, half)) for row in keep]
    for j in range(partners):
        weight = gate(pairing_ref, j, partners)
        gates_ref[j] = jnp.full(gates_ref.shape[1:], weight, jnp.float32)
        for a in range(tiles):
            keep_ref[j, a * half : (a + 1) * half] = columns[a] * weight
    for k, copy in enumerate(waits):
        copy.wait()
        stage[k % STAGES] = cot_ref[k].astype(jnp.float32).reshape(LEVELS * tiles, half)
        for a in range(tiles):
            w = relative(neighbours_ref, a, k, first)
            totals[a][w, :LEVELS] += stage[k % STAGES, pl.ds(a, LEVELS, stride=tiles), :]
    for a in range(tiles):
        for w in range(SPAN):
            coarse = totals[a][w, PIXELS:].astype(jnp.bfloat16)
            spread = jnp.dot(pool, coarse, preferred_element_type=jnp.float32)
            folded_ref[fold_rows(a, w)] = ((totals[a][w, :PIXELS] + spread) * keep[a]).astype(jnp.bfloat16)
    features_copy.wait()
    list_copy.wait()


def split(items, count):
    return items[:count], items[count:]


def fold_rows(a, w):
    start = (a * SPAN + w) * PIXELS
    return slice(start, start + PIXELS)


def fold(partners, neighbours, valid, pairing, cotangent, features):
    half = cotangent.shape[-1]
    _, tiles, pixels, channels = features.shape
    return call(
        functools.partial(fold_kernel, tiles, half, partners),
        "fold",
        (
            shape_of((tiles * SPAN * PIXELS, half)),
            shape_of((tiles, pixels, channels)),
            shape_of((partners, 8, channels), jnp.float32),
            shape_of((partners, tiles * half, channels), jnp.float32),
            shape_of((PAD, PIXELS)),
            shape_of(neighbours.shape, jnp.int32),
        ),
        [HBM] * 5,
        (VMEM,) * 6,
        [
            pltpu.SMEM(neighbours.shape, jnp.int32),
            pltpu.VMEM(valid.shape, jnp.int32),
            pltpu.SMEM(pairing.shape, jnp.int32),
            pltpu.VMEM(cotangent.shape, jnp.bfloat16),
            pltpu.VMEM((STAGES, LEVELS * tiles, half), jnp.float32),
            pltpu.SemaphoreType.DMA((5 + NEIGHBOURS,)),
        ]
        + [pltpu.VMEM((SPAN, WIDE, half), jnp.float32)] * tiles,
        10,
    )(*in_hbm(neighbours, valid, pairing, cotangent, features))


def halves(core, half):
    here = pl.ds(pl.multiple_of(core * half, half), half)
    there = pl.ds(pl.multiple_of((1 - core) * half, half), half)
    return here, there


def window_grad(tiles, slot, queries, folded_ref):
    users = [a for a in range(tiles) if 0 <= slot - a < SPAN]
    blocks = [folded_ref[fold_rows(a, slot - a)] for a in users]
    return jnp.dot(
        jnp.concatenate(blocks, axis=1),
        jnp.concatenate([queries[a] for a in users], axis=0),
        preferred_element_type=jnp.float32,
    )


def early_kernel(tiles, half, x_ref, mine_ref, part_ref):
    here, _ = halves(lax.axis_index("chan"), half)
    queries = [x_ref[a, here, :] for a in range(tiles)]
    for slot in range(3 * tiles):
        part_ref[slot] = window_grad(tiles, slot, queries, mine_ref)


def early(x, mine):
    tiles, pixels, channels = x.shape
    return call(
        functools.partial(early_kernel, tiles, mine.shape[1]),
        "early",
        shape_of((3 * tiles, pixels, channels), jnp.float32),
        [VMEM] * 2,
        VMEM,
        [],
        4,
    )(x, mine)


def keys_kernel(tiles, half, x_ref, part_ref, other_ref, own_ref, even_ref, odd_ref):
    _, there = halves(lax.axis_index("chan"), half)
    queries = [x_ref[a, there, :] for a in range(tiles)]

    def of_slot(slot):
        return part_ref[slot] + window_grad(tiles, slot, queries, other_ref)

    parity = lax.rem(lax.axis_index("tile"), 2)
    for a in range(tiles):
        below = of_slot(a).astype(jnp.bfloat16)
        above = of_slot(2 * tiles + a).astype(jnp.bfloat16)
        even_ref[a] = jnp.where(parity == 0, above, below)
        odd_ref[a] = jnp.where(parity == 0, below, above)
        own_ref[a] = of_slot(tiles + a)


def keys(x, part, other):
    tiles, half = x.shape[0], other.shape[1]
    return call(
        functools.partial(keys_kernel, tiles, half),
        "keys",
        (shape_of(x.shape, jnp.float32), shape_of(x.shape), shape_of(x.shape)),
        [VMEM] * 3,
        (VMEM,) * 3,
        [],
        4,
    )(x, part, other)


def returns_kernel(partners, gates_ref, own_ref, even_ref, odd_ref, *out_refs):
    tile, count = lax.axis_index("tile"), lax.axis_size("tile")
    parity = lax.rem(tile, 2)
    has_even = jnp.logical_or(parity == 1, tile + 1 < count)
    has_odd = jnp.logical_or(jnp.logical_and(parity == 0, tile > 0), jnp.logical_and(parity == 1, tile + 1 < count))
    tiles, pixels, _ = own_ref.shape
    for a in range(tiles):
        total = own_ref[a]
        total = total + jnp.where(has_even, even_ref[a].astype(jnp.float32), 0.0)
        total = total + jnp.where(has_odd, odd_ref[a].astype(jnp.float32), 0.0)
        for j in range(partners):
            out_refs[j][a * pixels : (a + 1) * pixels] = (total * gates_ref[j, :1]).astype(jnp.bfloat16)
    for j in range(partners):
        out_refs[j][tiles * pixels :] = jnp.zeros((MARGIN, out_refs[j].shape[1]), jnp.bfloat16)


def returns(partners, gates, own, even, odd):
    tiles, pixels, channels = own.shape
    return call(
        functools.partial(returns_kernel, partners),
        "returns",
        (shape_of((tiles * pixels + MARGIN, channels)),) * partners,
        [VMEM] * 4,
        (VMEM,) * partners,
        [],
        3,
    )(gates, own, even, odd)


def join(mine, other):
    core = lax.axis_index("chan")
    return jnp.concatenate([jnp.where(core == 0, mine, other), jnp.where(core == 0, other, mine)], axis=-1)


def multiply(left, right, contract):
    return lax.dot_general(left, right, ((contract[:1], contract[1:]), ((), ())), preferred_element_type=jnp.float32)


def query_grads(gates_ref, folded_ref, other_ref, tiles, partners, level_of, slots):
    grads = []
    for a in range(tiles):
        grad = None
        for j in range(partners):
            term = None
            for slot in slots:
                if 0 <= slot - a < SPAN:
                    rows = fold_rows(a, slot - a)
                    both = jnp.concatenate([folded_ref[rows], other_ref[rows]], axis=1)
                    part = multiply(both, level_of(j, slot), (0, 0))
                    term = part if term is None else term + part
            term = term * gates_ref[j, :1]
            grad = term if grad is None else grad + term
        grads.append(grad)
    return grads


def ready_kernel(tiles, half, partners, gates_ref, keep_ref, x_ref, xo_ref, folded_ref, other_ref, *refs):
    same, (queries_ref, grad_ref) = refs[:partners], refs[partners:]
    here, _ = halves(lax.axis_index("chan"), half)
    mine = jnp.concatenate([x_ref[a, here, :] for a in range(tiles)], axis=0).astype(jnp.float32)
    other = jnp.concatenate([xo_ref[a, here, :] for a in range(tiles)], axis=0).astype(jnp.float32)
    for j in range(partners):
        queries_ref[j] = join(mine * keep_ref[j], other * keep_ref[j]).T.astype(jnp.bfloat16)
    slots = range(tiles, 2 * tiles)
    grads = query_grads(
        gates_ref, folded_ref, other_ref, tiles, partners, lambda j, slot: same[j][slot - tiles], slots
    )
    for a in range(tiles):
        grad_ref[a] = grads[a]


def ready(partners, gates, keep, x, xo, folded, other, same):
    tiles, pixels, channels = x.shape
    return call(
        functools.partial(ready_kernel, tiles, pixels // 2, partners),
        "ready",
        (shape_of((partners, 2 * channels, tiles * pixels // 2)), shape_of(x.shape, jnp.float32)),
        [VMEM] * (6 + len(same)),
        (VMEM,) * 2,
        [],
        6,
    )(gates, keep, x, xo, folded, other, *same)


def sides_kernel(tiles, half, partners, gates_ref, folded_ref, other_ref, part_ref, *refs):
    inputs, (grad_ref, levels) = refs[: 2 * partners], refs[2 * partners :]
    here, there = halves(lax.axis_index("chan"), half)
    for j in range(partners):
        for part, base in enumerate(side_bases(tiles)):
            levels[j, pl.ds(base, tiles)] = inputs[2 * j + part][...]
    slots = [slot for slot in range(3 * tiles) if not tiles <= slot < 2 * tiles]
    grads = query_grads(
        gates_ref, folded_ref, other_ref, tiles, partners, lambda j, slot: levels[j, slot], slots
    )
    for a in range(tiles):
        grad = part_ref[a] + grads[a]
        grad_ref[a, here, :] = grad[:half]
        grad_ref[a, there, :] = grad[half:]


def sides(partners, gates, folded, other, part, windows):
    tiles, pixels, channels = windows[0].shape
    return call(
        functools.partial(sides_kernel, tiles, pixels // 2, partners),
        "sides",
        shape_of(windows[0].shape, jnp.float32),
        [VMEM] * (4 + len(windows)),
        VMEM,
        [pltpu.VMEM((partners, 3 * tiles, pixels, channels), jnp.bfloat16)],
        6,
    )(gates, folded, other, part, *windows)


def near_kernel(tiles, partners, queries_ref, pool_ref, *refs):
    same, (fine_ref, coarse_ref) = refs[: 2 * partners], refs[2 * partners :]
    pool = pool_ref[...]
    for s in range(tiles):
        fine, coarse = None, None
        for j in range(partners):
            level = join(same[2 * j][s], same[2 * j + 1][s])
            cells = jnp.dot(pool, level, preferred_element_type=jnp.float32).astype(jnp.bfloat16)
            fine_term = multiply(level, queries_ref[j], (1, 0))
            coarse_term = multiply(cells, queries_ref[j], (1, 0))
            fine = fine_term if fine is None else fine + fine_term
            coarse = coarse_term if coarse is None else coarse + coarse_term
        fine_ref[s] = fine
        coarse_ref[s] = coarse


def near(partners, queries, pool, same):
    tiles, pixels, _ = same[0].shape
    return call(
        functools.partial(near_kernel, tiles, partners),
        "near",
        (
            shape_of((tiles, pixels, tiles * pixels // 2), jnp.float32),
            shape_of((tiles, PAD, tiles * pixels // 2), jnp.float32),
        ),
        [VMEM] * (2 + len(same)),
        (VMEM,) * 2,
        [],
        6,
    )(queries, pool, *same)


def tables_kernel(tiles, partners, queries_ref, pool_ref, near_fine, near_coarse, *refs):
    inputs, (fine_table, coarse_table, levels, cells) = refs[: 4 * partners], refs[4 * partners :]
    fine_table[tiles : 2 * tiles] = near_fine[...]
    coarse_table[tiles : 2 * tiles] = near_coarse[...]
    pool = pool_ref[...]
    for j in range(partners):
        for part in range(2):
            for a in range(tiles):
                level = join(inputs[4 * j + part][a], inputs[4 * j + 2 + part][a])
                at = part * tiles + a
                levels[j, at * PIXELS : (at + 1) * PIXELS] = level
                cells[j, at * PAD : (at + 1) * PAD] = jnp.dot(
                    pool, level, preferred_element_type=jnp.float32
                ).astype(jnp.bfloat16)
    for keys_at, table in ((levels, fine_table), (cells, coarse_table)):
        scores = multiply(keys_at[0], queries_ref[0], (1, 0))
        for j in range(1, partners):
            scores = scores + multiply(keys_at[j], queries_ref[j], (1, 0))
        scores = scores.reshape(2, tiles, table.shape[1], table.shape[2])
        for part, base in enumerate(side_bases(tiles)):
            table[pl.ds(base, tiles)] = scores[part]


def tables(partners, queries, pool, fine, coarse, beside):
    tiles, pixels, channels = beside[0].shape
    return call(
        functools.partial(tables_kernel, tiles, partners),
        "tables",
        tuple(shape_of((3 * tiles,) + near.shape[1:], jnp.float32) for near in (fine, coarse)),
        [VMEM] * (4 + len(beside)),
        (VMEM,) * 2,
        [
            pltpu.VMEM((partners, 2 * tiles * pixels, 2 * channels), jnp.bfloat16),
            pltpu.VMEM((partners, 2 * tiles * PAD, 2 * channels), jnp.bfloat16),
        ],
        7,
    )(queries, pool, fine, coarse, *beside)


def volume_kernel(tiles, half, partners, list_ref, part_ref, fine_table, coarse_table, *refs):
    returned, (volume_hbm, grad_hbm, stage, volume_ref, grad_ref, sems) = refs[:partners], refs[partners:]
    first = lax.axis_index("tile") * tiles
    listed = list_ref[...]
    pixels, channels = grad_ref.shape[1:]
    waits = []
    for i_part, (entries, start, size) in enumerate(entry_pairs(tiles)):
        for i, k in enumerate(entries):
            for a in range(tiles):
                slot = relative(listed, a, k, first) + a
                lanes = slice(a * half, (a + 1) * half)
                base = i * LEVELS * tiles + a
                stage[pl.ds(base, PIXELS, stride=tiles), :] = fine_table[slot, :, lanes]
                stage[pl.ds(base + PIXELS * tiles, COARSE, stride=tiles), :] = coarse_table[slot, :COARSE, lanes]
        rows = pl.ds(start, size)
        volume_ref[rows, :] = stage[:size].astype(jnp.bfloat16)
        copy = pltpu.make_async_copy(volume_ref.at[rows], volume_hbm.at[rows], sems.at[1 + i_part])
        copy.start()
        waits.append(copy)
        if i_part == 1:
            for a in range(tiles):
                summed = part_ref[a]
                for j in range(partners):
                    summed = summed + returned[j][a * pixels : (a + 1) * pixels].astype(jnp.float32)
                grad_ref[a] = summed
            copy = pltpu.make_async_copy(grad_ref, grad_hbm.at[0], sems.at[0])
            copy.start()
            waits.append(copy)
    for copy in waits:
        copy.wait()


def volumes(partners, neighbours, grad, fine, coarse, returned):
    tiles, pixels, _ = grad.shape
    half = pixels // 2
    rows = NEIGHBOURS * LEVELS * tiles
    return call(
        functools.partial(volume_kernel, tiles, half, partners),
        "volume",
        (shape_of((rows, half)), shape_of((1,) + grad.shape, jnp.float32)),
        [VMEM] * (4 + len(returned)),
        (HBM, HBM),
        [
            pltpu.VMEM((2 * LEVELS * tiles, half), jnp.float32),
            pltpu.VMEM((rows, half), jnp.bfloat16),
            pltpu.VMEM(grad.shape, jnp.float32),
            pltpu.SemaphoreType.DMA((1 + (NEIGHBOURS + 1) // 2,)),
        ],
        8,
    )(neighbours, grad, fine, coarse, *returned)


def after(value, earlier):
    return lax.optimization_barrier((value, earlier))[0]


def local(features, neighbours, pairing, valid_tiles, cotangent):
    count = lax.axis_size("tile")
    cores = lax.axis_size("chan")
    links = frame_links(lax.axis_size("frame"))
    partners = len(links)
    tiles, half = cotangent.shape[1:3]
    swap = [(c, (c + 1) % cores) for c in range(cores)]
    evens, odds = even_pairs(count), odd_pairs(count, cores)

    def over_even(z):
        return lax.ppermute(z, "tile", evens)

    def over_odd(z):
        return lax.ppermute(z, ("tile", "chan"), odds)

    def over_cores(z):
        return lax.ppermute(z, "chan", swap)

    upstream = jnp.transpose(cotangent[0], (2, 0, 1)).reshape(NEIGHBOURS, LEVELS * tiles // 8, 8, half)
    folded, x, gates, keep, pool, listed = fold(partners, neighbours, valid_tiles, pairing, upstream, features)
    other = over_cores(folded)
    arrived = [lax.ppermute(x, "frame", ahead) for ahead, _ in links]
    own, to_even, to_odd = keys(x, early(x, folded), other)
    xo = over_cores(x)
    arrived = [after(y, own) for y in arrived]
    beside = [(over_even(y), over_odd(y)) for y in arrived]
    from_odd = over_odd(to_odd)
    from_even = after(over_even(to_even), from_odd)
    sent = returns(partners, gates, own, from_even, from_odd)
    returned = [lax.ppermute(z, "frame", back) for z, (_, back) in zip(sent, links, strict=True)]
    queries, part = ready(partners, gates, keep, x, xo, folded, other, [after(y, sent[0]) for y in arrived])
    same, mine, exchanged = [], [], []
    for y, (even, odd) in zip(arrived, beside, strict=True):
        even, odd = after(even, part), after(odd, part)
        same += [after(y, odd), after(over_cores(y), odd)]
        mine += [even, odd]
        exchanged += [even, odd, over_cores(even), over_cores(odd)]
    grad = sides(partners, gates, folded, other, part, mine)
    fine, coarse = near(partners, queries, pool, [after(z, grad) for z in same])
    exchanged = [after(after(z, grad), fine) for z in exchanged]
    fine, coarse = tables(partners, queries, pool, fine, coarse, exchanged)
    returned = [after(z, fine) for z in returned]
    volume, feature_grad = volumes(partners, listed, grad, fine, coarse, returned)
    volume = jnp.transpose(volume.reshape(NEIGHBOURS * LEVELS, tiles, half), (1, 2, 0))
    return volume[None], feature_grad


def solution(mesh):
    return jax.shard_map(
        local,
        mesh=mesh,
        in_specs=(
            P(("clip", "frame"), "tile", None, "chan"),
            P(("clip", "tile"), None),
            P(("clip", "frame"), None),
            P(("clip", "tile"), None),
            P(("clip", "frame"), "tile", "chan", None),
        ),
        out_specs=(
            P(("clip", "frame"), "tile", "chan", None),
            P(("clip", "frame"), "tile", None, "chan"),
        ),
        check_vma=False,
    )
```
